32 devices in a mesh: row: 4 (over x, core), col: 8 (over z, y).
Axes of the slice: x: 2, y: 2, z: 4, core: 2. Of those that a mesh axis runs over, the one named last changes fastest.
Arguments:
- density: float32 [2048, 2048], P('row', 'col'), may hold values from -0.4375 to 0.4375
- occupancy: int32 [16, 16], P('row', 'col'), may hold values from 0 to 1, as said below
Outputs:
- purified: float32 [2048, 2048], P('row', 'col')
The draws below stay inside these ranges and needn't reach their ends.
Inputs may be any that keep to these rules, and one draw needn't show every extreme that they name: `occupancy`: 1 marks an occupied 128 x 128 tile, 0 an empty one; every diagonal tile is occupied.
All inputs are finite; a program needn't handle non-finite values.
Results may differ from the reference program's by a relative error of at most 0.0001.
Values sent between devices are 32-bit elements; how exact they have to be, the bound alone decides.
A program may use at most 64 MiB of HBM per device.

```python
import jax
import jax.numpy as jnp
from jax import lax

BLK = 512
TILE = 128
SECTIONS = 3
ORDER = 2048


def draw_occupancy(key, part):
    tiles = ORDER // TILE
    grid_rows = ORDER // BLK
    grid_cols = 2 * grid_rows
    level_key = jax.random.fold_in(key, 11)
    tile_key = jax.random.fold_in(key, 23)
    levels = jax.random.randint(level_key, (grid_rows, grid_cols), 1, 4)
    per_tile = jnp.repeat(jnp.repeat(levels, BLK // TILE, axis=0), BLK // 2 // TILE, axis=1)
    rolls = jax.random.randint(tile_key, (tiles, tiles), 0, 3)
    occupied = jnp.where(rolls < per_tile, 1, 0).astype(jnp.int32)
    diagonal_tiles = jnp.eye(tiles, dtype=jnp.int32)
    return jnp.maximum(occupied, diagonal_tiles)


def level_of(stream_key, shape, pieces, least, top_value):
    level, own = 1.0, jax.random.fold_in(stream_key, 6)
    for position, blocks in pieces:
        draws = jnp.exp(jax.random.uniform(jax.random.fold_in(own, position), (blocks,), jnp.float32, least / len(pieces), top_value / len(pieces)))
        level = level * jnp.repeat(draws, shape[position] // blocks).reshape([-1 if axis == position else 1 for axis in range(len(shape))])
    return level


def noise(own_key, dims, scale, most, pieces=(), held_as=jnp.bfloat16):
    level = level_of(own_key, dims, pieces, -0.22, 0.18) if pieces else 1.0
    array = jax.random.normal(own_key, dims, jnp.float32) * scale * level
    return jnp.minimum(jnp.maximum(array, -most), most).astype(held_as)


def setup_inputs(seed: int = 0) -> dict:
    seeds = jax.random.split(jax.random.key(seed), 3)
    density = noise(seeds[0], (ORDER, ORDER), (3 * BLK // 8) ** -0.5, 0.4375, ((0, 4), (1, 8)), jnp.float32)
    occupancy = draw_occupancy(jax.random.fold_in(seeds[2], 71), 0)
    return dict(density=density, occupancy=occupancy)


def expand(occupancy):
    wide = jnp.repeat(jnp.repeat(occupancy, TILE, axis=0), TILE, axis=1)
    return wide.astype(jnp.float32)


def windowed(left, right):
    block_count = ORDER // BLK
    left_grid = left.reshape(block_count, BLK, block_count, BLK)
    right_grid = right.reshape(block_count, BLK, ORDER)
    rows_index = jnp.arange(block_count)
    accum = jnp.zeros((block_count, BLK, ORDER), jnp.float32)
    for section_index in range(SECTIONS):
        diag_blocks = left_grid[rows_index, :, (rows_index + section_index) % block_count, :]
        shifted = jnp.roll(right_grid, -section_index, axis=0)
        accum = accum + jnp.einsum("rij,rjn->rin", diag_blocks, shifted, precision=lax.Precision.HIGHEST)
    return accum.reshape(ORDER, ORDER)


def reference(density, occupancy):
    mask = expand(occupancy)
    masked = density * mask
    square_term = windowed(masked, masked) * mask
    cube_term = windowed(masked, square_term) * mask
    return 3.0 * square_term - 2.0 * cube_term
```

```python
import functools

import jax
import jax.numpy as jnp
from jax import lax
from jax.experimental import pallas as pl
from jax.experimental.pallas import tpu as pltpu
from jax.sharding import PartitionSpec as P

SECTIONS = 3
CHUNKS = 4
ROW_TILE = 128
MESH = pl.DeviceIdType.MESH


def split(values):
    high = values.astype(jnp.bfloat16)
    low = (values - high.astype(jnp.float32)).astype(jnp.bfloat16)
    return high, low


def product(left_high, left_low, right_high, right_low):
    dot = functools.partial(jnp.dot, preferred_element_type=jnp.float32)
    return dot(left_high, right_high) + (dot(left_high, right_low) + dot(left_low, right_high))


def kernel(
    row_count, col_count, occ_ref, den_ref, out_ref,
    left, left_high, left_low, right, square, right_high, right_low, cube,
    left_recv, z_send, y_send, right_recv, right_send, square_recv, square_send,
):
    blk, half_cols = den_ref.shape
    rows = blk // CHUNKS
    tile_rows, tile_cols = occ_ref.shape
    tr, tc = blk // tile_rows, half_cols // tile_cols
    block_count = col_count // 2

    r, c = lax.axis_index("row"), lax.axis_index("col")
    place, half = lax.div(c, 2), lax.rem(c, 2)
    other = 1 - half
    core = lax.rem(r, 2)
    partner = c + 1 - 2 * half
    buddy = r + 1 - 2 * core
    above = lax.rem(r + row_count - 2, row_count)
    below = lax.rem(r + 2, row_count)
    has_prev, has_next = place > 0, place < block_count - 1
    own_section = lax.rem(place - r + block_count, block_count)

    barrier = pltpu.get_barrier_semaphore()

    def greet(**device):
        pl.semaphore_signal(barrier, inc=1, device_id=device, device_id_type=MESH)

    @pl.when(has_prev)
    def _():
        greet(col=c - 2)

    @pl.when(has_next)
    def _():
        greet(col=c + 2)

    greet(col=partner)
    greet(row=buddy)
    greet(row=above)
    if row_count > 4:
        greet(row=below)

    def masked_by_tiles(values, first_tile_row, count):
        lines = []
        for i in range(count):
            line = []
            for k in range(tile_cols):
                weight = occ_ref[first_tile_row + i, k].astype(jnp.float32)
                line.append(values[i * tr : (i + 1) * tr, k * tc : (k + 1) * tc] * weight)
            lines.append(jnp.concatenate(line, axis=1))
        return jnp.concatenate(lines, axis=0)

    for i in range(tile_rows):
        part = masked_by_tiles(den_ref[i * tr : (i + 1) * tr, :], i, 1)
        right[0, i * tr : (i + 1) * tr, :] = part

        @pl.when(own_section < SECTIONS)
        def _():
            left[own_section, half, i * tr : (i + 1) * tr, :] = part

    pl.semaphore_wait(
        barrier,
        has_prev.astype(jnp.int32) + has_next.astype(jnp.int32) + (4 if row_count > 4 else 3),
    )

    def left_copy(section, side, chunk, send_sem, **device):
        piece = left.at[section, side, pl.ds(chunk * rows, rows), :]
        return pltpu.make_async_remote_copy(
            src_ref=piece, dst_ref=piece, send_sem=send_sem,
            recv_sem=left_recv.at[section, side, chunk],
            device_id=device, device_id_type=MESH,
        )

    def spread(section, chunk, to_prev, to_next):
        if to_prev:
            @pl.when(has_prev)
            def _():
                left_copy(section, half, chunk, z_send.at[0, section], col=c - 2).start()

        if to_next:
            @pl.when(has_next)
            def _():
                left_copy(section, half, chunk, z_send.at[1, section], col=c + 2).start()

        left_copy(section, half, chunk, y_send.at[section], col=partner).start()

    def wait_left(section, side, chunk):
        left_copy(section, side, chunk, y_send.at[section], col=partner).wait_recv()

    def send_own(chunk):
        @pl.when(own_section < SECTIONS)
        def _():
            spread(own_section, chunk, True, True)

    def forward(chunk):
        if chunk + 1 < CHUNKS:
            send_own(chunk + 1)

        def step(distance, carry):
            for sign in (-1, 1):
                source = place + sign * distance
                section = lax.rem(source - r + 2 * block_count, block_count)
                inside = source >= 0 if sign < 0 else source < block_count

                @pl.when(jnp.logical_and(inside, section < SECTIONS))
                def _():
                    wait_left(section, half, chunk)
                    spread(section, chunk, sign > 0, sign < 0)

            return carry

        lax.fori_loop(1, block_count, step, 0)

    def right_copy(buffer, from_slot, to_slot, chunk, send_sem, recv_sems, device_row):
        span = pl.ds(chunk * rows, rows)
        return pltpu.make_async_remote_copy(
            src_ref=buffer.at[from_slot, span, :], dst_ref=buffer.at[to_slot, span, :],
            send_sem=send_sem, recv_sem=recv_sems.at[to_slot - 1, chunk],
            device_id={"row": device_row}, device_id_type=MESH,
        )

    def send_right(buffer, chunk, send_sems, recv_sems):
        right_copy(buffer, 0, 2, chunk, send_sems.at[0], recv_sems, above).start()

        @pl.when(core == 1)
        def _():
            right_copy(buffer, 0, 1, chunk, send_sems.at[1], recv_sems, buddy).start()

    def relay_right(buffer, chunk, send_sems, recv_sems):
        right_copy(buffer, 0, 2, chunk, send_sems.at[0], recv_sems, above).wait_recv()

        @pl.when(core == 0)
        def _():
            right_copy(buffer, 2, 1, chunk, send_sems.at[1], recv_sems, buddy).start()

    def wait_next(buffer, chunk, send_sems, recv_sems):
        right_copy(buffer, 0, 1, chunk, send_sems.at[1], recv_sems, buddy).wait_recv()

    def split_right(buffer, slot, first, count):
        high, low = split(buffer[slot, first : first + count, :])
        right_high[slot, first : first + count, :] = high
        right_low[slot, first : first + count, :] = low

    def consume(chunk):
        span = slice(chunk * rows, (chunk + 1) * rows)
        for section in range(SECTIONS):
            wait_left(section, other, chunk)
        total = jnp.zeros((rows, half_cols), jnp.float32)
        for section in range(SECTIONS):
            for side in range(2):
                high, low = split(left[section, side, span, :])
                left_high[section, side, span, :] = high
                left_low[section, side, span, :] = low
                depth = slice(side * half_cols, (side + 1) * half_cols)
                total = total + product(
                    high, low, right_high[section, depth, :], right_low[section, depth, :]
                )
        tiles = rows // tr
        square[0, span, :] = masked_by_tiles(total, chunk * tiles, tiles)
        send_right(square, chunk, square_send, square_recv)

    for chunk in range(CHUNKS):
        send_right(right, chunk, right_send, right_recv)
    send_own(0)

    for step in range(CHUNKS + 1):
        if step < CHUNKS:
            forward(step)
        if step == 1:
            for chunk in range(CHUNKS):
                relay_right(right, chunk, right_send, right_recv)
            split_right(right, 0, 0, blk)
            split_right(right, 2, 0, blk)
            for chunk in range(CHUNKS):
                wait_next(right, chunk, right_send, right_recv)
            split_right(right, 1, 0, blk)
        if step >= 1:
            consume(step - 1)
        if step >= 2:
            relay_right(square, step - 2, square_send, square_recv)

    def accumulate(terms, last):
        def step(tile, carry):
            span = pl.ds(pl.multiple_of(tile * ROW_TILE, ROW_TILE), ROW_TILE)
            total = cube[span, :] if last else jnp.zeros((ROW_TILE, half_cols), jnp.float32)
            for section, side in terms:
                depth = slice(side * half_cols, (side + 1) * half_cols)
                total = total + product(
                    left_high[section, side, span, :], left_low[section, side, span, :],
                    right_high[section, depth, :], right_low[section, depth, :],
                )
            cube[span, :] = total
            return carry

        lax.fori_loop(0, blk // ROW_TILE, step, 0)

    split_right(square, 0, 0, blk)
    for chunk in range(CHUNKS // 2):
        wait_next(square, chunk, square_send, square_recv)
    split_right(square, 1, 0, half_cols)
    split_right(square, 2, 0, half_cols)
    accumulate([(0, 0), (0, 1), (1, 0), (2, 0)], False)
    relay_right(square, CHUNKS - 1, square_send, square_recv)
    split_right(square, 2, half_cols, half_cols)
    for chunk in range(CHUNKS // 2, CHUNKS):
        wait_next(square, chunk, square_send, square_recv)
    split_right(square, 1, half_cols, half_cols)
    accumulate([(1, 1), (2, 1)], True)

    for i in range(tile_rows):
        span = slice(i * tr, (i + 1) * tr)
        out_ref[span, :] = 3.0 * square[0, span, :] - 2.0 * masked_by_tiles(cube[span, :], i, 1)

    def all_sent(whole, send_sem):
        pltpu.make_async_copy(whole, whole, send_sem).wait()

    for section in range(SECTIONS):
        source = lax.rem(r + section, block_count)
        whole = left.at[section, half]

        @pl.when(jnp.logical_and(has_prev, source >= place))
        def _():
            all_sent(whole, z_send.at[0, section])

        @pl.when(jnp.logical_and(has_next, source <= place))
        def _():
            all_sent(whole, z_send.at[1, section])

        all_sent(whole, y_send.at[section])
    for sems in (right_send, square_send):
        for k in range(2):
            all_sent(right.at[0], sems.at[k])


def per_device(density, occupancy):
    blk, half_cols = density.shape
    row_count, col_count = lax.axis_size("row"), lax.axis_size("col")
    dma = pltpu.SemaphoreType.DMA
    wide = (SECTIONS, 2, blk, half_cols)
    tall = (SECTIONS, blk, half_cols)
    flops = 12 * blk * SECTIONS * blk * half_cols
    return pl.pallas_call(
        functools.partial(kernel, row_count, col_count),
        out_shape=jax.ShapeDtypeStruct(density.shape, jnp.float32),
        in_specs=[
            pl.BlockSpec(memory_space=pltpu.SMEM),
            pl.BlockSpec(memory_space=pltpu.VMEM),
        ],
        out_specs=pl.BlockSpec(memory_space=pltpu.VMEM),
        scratch_shapes=[
            pltpu.VMEM(wide, jnp.float32),
            pltpu.VMEM(wide, jnp.bfloat16),
            pltpu.VMEM(wide, jnp.bfloat16),
            pltpu.VMEM(tall, jnp.float32),
            pltpu.VMEM(tall, jnp.float32),
            pltpu.VMEM(tall, jnp.bfloat16),
            pltpu.VMEM(tall, jnp.bfloat16),
            pltpu.VMEM((blk, half_cols), jnp.float32),
            dma((SECTIONS, 2, CHUNKS)),
            dma((2, SECTIONS)),
            dma((SECTIONS,)),
            dma((2, CHUNKS)),
            dma((2,)),
            dma((2, CHUNKS)),
            dma((2,)),
        ],
        compiler_params=pltpu.CompilerParams(
            collective_id=0, has_side_effects=True, vmem_limit_bytes=40 * 2**20
        ),
        cost_estimate=pl.CostEstimate(
            flops=flops, bytes_accessed=2 * 4 * blk * half_cols, transcendentals=0
        ),
    )(occupancy, density)


def solution(mesh):
    in_specs = (P("row", "col"), P("row", "col"))
    out_specs = P("row", "col")
    return jax.shard_map(
        per_device, mesh=mesh, in_specs=in_specs, out_specs=out_specs, check_vma=False
    )
```

```python
import functools

import jax
import jax.numpy as jnp
from jax import lax
from jax.experimental import pallas as pl
from jax.experimental.pallas import tpu as pltpu
from jax.sharding import PartitionSpec as P

SECTIONS = 3
CHUNKS = 8
ROW_TILE = 128
MESH = pl.DeviceIdType.MESH


def split(values):
    high = values.astype(jnp.bfloat16)
    low = (values - high.astype(jnp.float32)).astype(jnp.bfloat16)
    return high, low


def product(left_high, left_low, right_high, right_low):
    dot = functools.partial(jnp.dot, preferred_element_type=jnp.float32)
    count = left_high.shape[0]
    both = dot(jnp.concatenate([left_high, left_low], axis=0), right_high)
    return both[:count] + (both[count:] + dot(left_high, right_low))


def kernel(
    row_count, col_count, occ_ref, den_ref, out_ref,
    left, left_high, left_low, right, square, right_high, right_low, cube,
    left_recv, z_send, y_send, right_recv, right_send, square_recv, square_send, load_sem,
):
    blk, half_cols = den_ref.shape
    rows = blk // CHUNKS
    tile_cols, tile_rows = occ_ref.shape
    tr, tc = blk // tile_rows, half_cols // tile_cols
    block_count = col_count // 2

    r, c = lax.axis_index("row"), lax.axis_index("col")
    place, half = lax.div(c, 2), lax.rem(c, 2)
    other = 1 - half
    core = lax.rem(r, 2)
    partner = c + 1 - 2 * half
    buddy = r + 1 - 2 * core
    above = lax.rem(r + row_count - 2, row_count)
    below = lax.rem(r + 2, row_count)
    has_prev, has_next = place > 0, place < block_count - 1
    own_section = lax.rem(place - r + block_count, block_count)

    load = pltpu.make_async_copy(den_ref, cube, load_sem)
    load.start()

    barrier = pltpu.get_barrier_semaphore()

    def greet(**device):
        pl.semaphore_signal(barrier, inc=1, device_id=device, device_id_type=MESH)

    @pl.when(has_prev)
    def _():
        greet(col=c - 2)

    @pl.when(has_next)
    def _():
        greet(col=c + 2)

    greet(col=partner)
    greet(row=buddy)
    greet(row=above)
    if row_count > 4:
        greet(row=below)

    def masked_by_tiles(values, first_row):
        count = min(tr, values.shape[0])
        lines = []
        for i in range(0, values.shape[0], count):
            line = []
            for k in range(tile_cols):
                weight = occ_ref[k, (first_row + i) // tr].astype(jnp.float32)
                line.append(values[i : i + count, k * tc : (k + 1) * tc] * weight)
            lines.append(jnp.concatenate(line, axis=1))
        return jnp.concatenate(lines, axis=0)

    load.wait()
    for i in range(tile_rows):
        part = masked_by_tiles(cube[i * tr : (i + 1) * tr, :], i * tr)
        right[0, i * tr : (i + 1) * tr, :] = part

        @pl.when(own_section < SECTIONS)
        def _():
            left[own_section, half, i * tr : (i + 1) * tr, :] = part

    pl.semaphore_wait(
        barrier,
        has_prev.astype(jnp.int32) + has_next.astype(jnp.int32) + (4 if row_count > 4 else 3),
    )

    def left_copy(section, side, chunk, send_sem, **device):
        piece = left.at[section, side, pl.ds(chunk * rows, rows), :]
        return pltpu.make_async_remote_copy(
            src_ref=piece, dst_ref=piece, send_sem=send_sem,
            recv_sem=left_recv.at[section, side, chunk],
            device_id=device, device_id_type=MESH,
        )

    def spread(section, chunk, to_prev, to_next):
        if to_prev:
            @pl.when(has_prev)
            def _():
                left_copy(section, half, chunk, z_send.at[0, section], col=c - 2).start()

        if to_next:
            @pl.when(has_next)
            def _():
                left_copy(section, half, chunk, z_send.at[1, section], col=c + 2).start()

        left_copy(section, half, chunk, y_send.at[section], col=partner).start()

    def wait_left(section, side, chunk):
        left_copy(section, side, chunk, y_send.at[section], col=partner).wait_recv()

    def send_own(chunk):
        @pl.when(own_section < SECTIONS)
        def _():
            spread(own_section, chunk, True, True)

    def forward(chunk):
        if chunk + 1 < CHUNKS:
            send_own(chunk + 1)

        def step(distance, carry):
            for sign in (-1, 1):
                source = place + sign * distance
                section = lax.rem(source - r + 2 * block_count, block_count)
                inside = source >= 0 if sign < 0 else source < block_count

                @pl.when(jnp.logical_and(inside, section < SECTIONS))
                def _():
                    wait_left(section, half, chunk)
                    spread(section, chunk, sign > 0, sign < 0)

            return carry

        lax.fori_loop(1, block_count, step, 0)

    def right_copy(buffer, from_slot, to_slot, chunk, send_sem, recv_sems, device_row):
        span = pl.ds(chunk * rows, rows)
        return pltpu.make_async_remote_copy(
            src_ref=buffer.at[from_slot, span, :], dst_ref=buffer.at[to_slot, span, :],
            send_sem=send_sem, recv_sem=recv_sems.at[to_slot - 1, chunk],
            device_id={"row": device_row}, device_id_type=MESH,
        )

    def send_right(buffer, chunk, send_sems, recv_sems):
        right_copy(buffer, 0, 2, chunk, send_sems.at[0], recv_sems, above).start()

        @pl.when(core == 1)
        def _():
            right_copy(buffer, 0, 1, chunk, send_sems.at[1], recv_sems, buddy).start()

    def relay_right(buffer, chunk, send_sems, recv_sems):
        right_copy(buffer, 0, 2, chunk, send_sems.at[0], recv_sems, above).wait_recv()

        @pl.when(core == 0)
        def _():
            right_copy(buffer, 2, 1, chunk, send_sems.at[1], recv_sems, buddy).start()

    def wait_next(buffer, chunk, send_sems, recv_sems):
        right_copy(buffer, 0, 1, chunk, send_sems.at[1], recv_sems, buddy).wait_recv()

    def split_right(buffer, slot, first, count):
        high, low = split(buffer[slot, first : first + count, :])
        right_high[slot, first : first + count, :] = high
        right_low[slot, first : first + count, :] = low

    def consume(chunk):
        span = slice(chunk * rows, (chunk + 1) * rows)
        for section in range(SECTIONS):
            wait_left(section, other, chunk)
        total = jnp.zeros((rows, half_cols), jnp.float32)
        for section in range(SECTIONS):
            for side in range(2):
                high, low = split(left[section, side, span, :])
                left_high[section, side, span, :] = high
                left_low[section, side, span, :] = low
                depth = slice(side * half_cols, (side + 1) * half_cols)
                total = total + product(
                    high, low, right_high[section, depth, :], right_low[section, depth, :]
                )
        square[0, span, :] = masked_by_tiles(total, chunk * rows)
        send_right(square, chunk, square_send, square_recv)

    for chunk in range(CHUNKS):
        send_right(right, chunk, right_send, right_recv)
    send_own(0)

    for step in range(CHUNKS + 1):
        if step < CHUNKS:
            forward(step)
        if step == 1:
            for chunk in range(CHUNKS):
                relay_right(right, chunk, right_send, right_recv)
            split_right(right, 0, 0, blk)
            split_right(right, 2, 0, blk)
            for chunk in range(CHUNKS):
                wait_next(right, chunk, right_send, right_recv)
            split_right(right, 1, 0, blk)
        if step >= 1:
            consume(step - 1)
        if step >= 2:
            relay_right(square, step - 2, square_send, square_recv)

    def accumulate(terms, last):
        def step(tile, carry):
            span = pl.ds(pl.multiple_of(tile * ROW_TILE, ROW_TILE), ROW_TILE)
            total = cube[span, :] if last else jnp.zeros((ROW_TILE, half_cols), jnp.float32)
            for section, side in terms:
                depth = slice(side * half_cols, (side + 1) * half_cols)
                total = total + product(
                    left_high[section, side, span, :], left_low[section, side, span, :],
                    right_high[section, depth, :], right_low[section, depth, :],
                )
            cube[span, :] = total
            return carry

        lax.fori_loop(0, blk // ROW_TILE, step, 0)

    split_right(square, 0, 0, blk)
    for chunk in range(CHUNKS // 2):
        wait_next(square, chunk, square_send, square_recv)
    split_right(square, 1, 0, half_cols)
    split_right(square, 2, 0, half_cols)
    accumulate([(0, 0), (0, 1), (1, 0), (2, 0)], False)
    relay_right(square, CHUNKS - 1, square_send, square_recv)
    split_right(square, 2, half_cols, half_cols)
    for chunk in range(CHUNKS // 2, CHUNKS):
        wait_next(square, chunk, square_send, square_recv)
    split_right(square, 1, half_cols, half_cols)
    accumulate([(1, 1), (2, 1)], True)

    for i in range(tile_rows):
        span = slice(i * tr, (i + 1) * tr)
        out_ref[span, :] = 3.0 * square[0, span, :] - 2.0 * masked_by_tiles(cube[span, :], i * tr)

    def all_sent(whole, send_sem):
        pltpu.make_async_copy(whole, whole, send_sem).wait()

    for section in range(SECTIONS):
        source = lax.rem(r + section, block_count)
        whole = left.at[section, half]

        @pl.when(jnp.logical_and(has_prev, source >= place))
        def _():
            all_sent(whole, z_send.at[0, section])

        @pl.when(jnp.logical_and(has_next, source <= place))
        def _():
            all_sent(whole, z_send.at[1, section])

        all_sent(whole, y_send.at[section])
    for sems in (right_send, square_send):
        for k in range(2):
            all_sent(right.at[0], sems.at[k])


def per_device(density, occupancy):
    blk, half_cols = density.shape
    row_count, col_count = lax.axis_size("row"), lax.axis_size("col")
    dma = pltpu.SemaphoreType.DMA
    wide = (SECTIONS, 2, blk, half_cols)
    tall = (SECTIONS, blk, half_cols)
    flops = 12 * blk * SECTIONS * blk * half_cols
    return pl.pallas_call(
        functools.partial(kernel, row_count, col_count),
        out_shape=jax.ShapeDtypeStruct(density.shape, jnp.float32),
        in_specs=[
            pl.BlockSpec(memory_space=pltpu.SMEM),
            pl.BlockSpec(memory_space=pltpu.HBM),
        ],
        out_specs=pl.BlockSpec(memory_space=pltpu.VMEM),
        scratch_shapes=[
            pltpu.VMEM(wide, jnp.float32),
            pltpu.VMEM(wide, jnp.bfloat16),
            pltpu.VMEM(wide, jnp.bfloat16),
            pltpu.VMEM(tall, jnp.float32),
            pltpu.VMEM(tall, jnp.float32),
            pltpu.VMEM(tall, jnp.bfloat16),
            pltpu.VMEM(tall, jnp.bfloat16),
            pltpu.VMEM((blk, half_cols), jnp.float32),
            dma((SECTIONS, 2, CHUNKS)),
            dma((2, SECTIONS)),
            dma((SECTIONS,)),
            dma((2, CHUNKS)),
            dma((2,)),
            dma((2, CHUNKS)),
            dma((2,)),
            dma,
        ],
        compiler_params=pltpu.CompilerParams(
            collective_id=0, has_side_effects=True, vmem_limit_bytes=40 * 2**20
        ),
        cost_estimate=pl.CostEstimate(
            flops=flops, bytes_accessed=2 * 4 * blk * half_cols, transcendentals=0
        ),
    )(occupancy.T, density)


def solution(mesh):
    in_specs = (P("row", "col"), P("row", "col"))
    out_specs = P("row", "col")
    return jax.shard_map(
        per_device, mesh=mesh, in_specs=in_specs, out_specs=out_specs, check_vma=False
    )
```

```python
import functools

import jax
import jax.numpy as jnp
from jax import lax
from jax.experimental import pallas as pl
from jax.experimental.pallas import tpu as pltpu
from jax.sharding import PartitionSpec as P

SECTIONS = 3
CHUNKS = 8
GROUPS = ((0, 2), (2, 2), (4, 2), (6, 1), (7, 1))
AHEAD = 2
ROW_TILE = 128
MESH = pl.DeviceIdType.MESH


def split(values):
    high = values.astype(jnp.bfloat16)
    low = (values - high.astype(jnp.float32)).astype(jnp.bfloat16)
    return high, low


def product(left_high, left_low, right_high, right_low):
    dot = functools.partial(jnp.dot, preferred_element_type=jnp.float32)
    count = left_high.shape[0]
    both = dot(jnp.concatenate([left_high, left_low], axis=0), right_high)
    return both[:count] + (both[count:] + dot(left_high, right_low))


def kernel(
    row_count, col_count, occ_ref, den_ref, out_ref,
    left, left_high, left_low, right, square, right_high, right_low, cube,
    left_recv, z_send, y_send, right_recv, right_send, square_recv, square_send, load_sem,
):
    blk, half_cols = den_ref.shape
    rows = blk // CHUNKS
    tile_cols, tile_rows = occ_ref.shape
    tr, tc = blk // tile_rows, half_cols // tile_cols
    block_count = col_count // 2

    r, c = lax.axis_index("row"), lax.axis_index("col")
    place, half = lax.div(c, 2), lax.rem(c, 2)
    other = 1 - half
    core = lax.rem(r, 2)
    partner = c + 1 - 2 * half
    buddy = r + 1 - 2 * core
    above = lax.rem(r + row_count - 2, row_count)
    below = lax.rem(r + 2, row_count)
    has_prev, has_next = place > 0, place < block_count - 1
    own_section = lax.rem(place - r + block_count, block_count)

    load = pltpu.make_async_copy(den_ref, cube, load_sem)
    load.start()

    barrier = pltpu.get_barrier_semaphore()

    def greet(**device):
        pl.semaphore_signal(barrier, inc=1, device_id=device, device_id_type=MESH)

    @pl.when(has_prev)
    def _():
        greet(col=c - 2)

    @pl.when(has_next)
    def _():
        greet(col=c + 2)

    greet(col=partner)
    greet(row=buddy)
    greet(row=above)
    if row_count > 4:
        greet(row=below)

    def masked_by_tiles(values, first_row):
        count = min(tr, values.shape[0])
        lines = []
        for i in range(0, values.shape[0], count):
            line = []
            for k in range(tile_cols):
                weight = occ_ref[k, (first_row + i) // tr].astype(jnp.float32)
                line.append(values[i : i + count, k * tc : (k + 1) * tc] * weight)
            lines.append(jnp.concatenate(line, axis=1))
        return jnp.concatenate(lines, axis=0)

    load.wait()
    for i in range(tile_rows):
        part = masked_by_tiles(cube[i * tr : (i + 1) * tr, :], i * tr)
        right[0, i * tr : (i + 1) * tr, :] = part

        @pl.when(own_section < SECTIONS)
        def _():
            left[own_section, half, i * tr : (i + 1) * tr, :] = part

    pl.semaphore_wait(
        barrier,
        has_prev.astype(jnp.int32) + has_next.astype(jnp.int32) + (4 if row_count > 4 else 3),
    )

    def left_copy(section, side, chunk, send_sem, **device):
        piece = left.at[section, side, pl.ds(chunk * rows, rows), :]
        return pltpu.make_async_remote_copy(
            src_ref=piece, dst_ref=piece, send_sem=send_sem,
            recv_sem=left_recv.at[section, side, chunk],
            device_id=device, device_id_type=MESH,
        )

    def spread(section, chunk, to_prev, to_next):
        if to_prev:
            @pl.when(has_prev)
            def _():
                left_copy(section, half, chunk, z_send.at[0, section], col=c - 2).start()

        if to_next:
            @pl.when(has_next)
            def _():
                left_copy(section, half, chunk, z_send.at[1, section], col=c + 2).start()

        left_copy(section, half, chunk, y_send.at[section], col=partner).start()

    def wait_left(section, side, chunk):
        left_copy(section, side, chunk, y_send.at[section], col=partner).wait_recv()

    def send_own(chunk):
        @pl.when(own_section < SECTIONS)
        def _():
            spread(own_section, chunk, True, True)

    def forward(now):
        if now + AHEAD < CHUNKS:
            send_own(now + AHEAD)

        def step(distance, carry):
            chunk = now + 1 - distance
            for sign in (-1, 1):
                source = place + sign * distance
                section = lax.rem(source - r + 2 * block_count, block_count)
                inside = source >= 0 if sign < 0 else source < block_count

                @pl.when(jnp.logical_and(inside, section < SECTIONS))
                def _():
                    wait_left(section, half, chunk)
                    spread(section, chunk, sign > 0, sign < 0)

            return carry

        lax.fori_loop(max(1, now + 2 - CHUNKS), min(block_count - 1, now + 1) + 1, step, 0)

    def right_copy(buffer, from_slot, to_slot, chunk, send_sem, recv_sems, device_row):
        span = pl.ds(chunk * rows, rows)
        return pltpu.make_async_remote_copy(
            src_ref=buffer.at[from_slot, span, :], dst_ref=buffer.at[to_slot, span, :],
            send_sem=send_sem, recv_sem=recv_sems.at[to_slot - 1, chunk],
            device_id={"row": device_row}, device_id_type=MESH,
        )

    def send_right(buffer, chunk, send_sems, recv_sems):
        right_copy(buffer, 0, 2, chunk, send_sems.at[0], recv_sems, above).start()

        @pl.when(core == 1)
        def _():
            right_copy(buffer, 0, 1, chunk, send_sems.at[1], recv_sems, buddy).start()

    def relay_right(buffer, chunk, send_sems, recv_sems):
        right_copy(buffer, 0, 2, chunk, send_sems.at[0], recv_sems, above).wait_recv()

        @pl.when(core == 0)
        def _():
            right_copy(buffer, 2, 1, chunk, send_sems.at[1], recv_sems, buddy).start()

    def wait_next(buffer, chunk, send_sems, recv_sems):
        right_copy(buffer, 0, 1, chunk, send_sems.at[1], recv_sems, buddy).wait_recv()

    def split_right(buffer, slot, first, count):
        high, low = split(buffer[slot, first : first + count, :])
        right_high[slot, first : first + count, :] = high
        right_low[slot, first : first + count, :] = low

    def consume(first, count):
        span = slice(first * rows, (first + count) * rows)
        for chunk in range(first, first + count):
            for section in range(SECTIONS):
                wait_left(section, other, chunk)
        total = jnp.zeros((count * rows, half_cols), jnp.float32)
        for section in range(SECTIONS):
            for side in range(2):
                high, low = split(left[section, side, span, :])
                left_high[section, side, span, :] = high
                left_low[section, side, span, :] = low
                depth = slice(side * half_cols, (side + 1) * half_cols)
                total = total + product(
                    high, low, right_high[section, depth, :], right_low[section, depth, :]
                )
        square[0, span, :] = masked_by_tiles(total, first * rows)
        for chunk in range(first, first + count):
            send_right(square, chunk, square_send, square_recv)

    for chunk in range(CHUNKS):
        send_right(right, chunk, right_send, right_recv)
    for chunk in range(AHEAD):
        send_own(chunk)

    lag = block_count - 1
    pending = None
    for now in range(CHUNKS + lag):
        if now < CHUNKS + lag - 1:
            forward(now)
        done = [g for g in GROUPS if g[0] + g[1] - 1 + lag == now]
        if not done:
            continue
        if done[0][0] == 0:
            for chunk in range(CHUNKS):
                relay_right(right, chunk, right_send, right_recv)
            split_right(right, 0, 0, blk)
            split_right(right, 2, 0, blk)
            for chunk in range(CHUNKS):
                wait_next(right, chunk, right_send, right_recv)
            split_right(right, 1, 0, blk)
        consume(*done[0])
        if pending:
            for chunk in range(pending[0], sum(pending)):
                relay_right(square, chunk, square_send, square_recv)
        pending = done[0]

    def accumulate(terms, last):
        def step(tile, carry):
            span = pl.ds(pl.multiple_of(tile * ROW_TILE, ROW_TILE), ROW_TILE)
            total = cube[span, :] if last else jnp.zeros((ROW_TILE, half_cols), jnp.float32)
            for section, side in terms:
                depth = slice(side * half_cols, (side + 1) * half_cols)
                total = total + product(
                    left_high[section, side, span, :], left_low[section, side, span, :],
                    right_high[section, depth, :], right_low[section, depth, :],
                )
            cube[span, :] = total
            return carry

        lax.fori_loop(0, blk // ROW_TILE, step, 0)

    split_right(square, 0, 0, blk)
    for chunk in range(CHUNKS // 2):
        wait_next(square, chunk, square_send, square_recv)
    split_right(square, 1, 0, half_cols)
    split_right(square, 2, 0, half_cols)
    accumulate([(0, 0), (0, 1), (1, 0), (2, 0)], False)
    relay_right(square, CHUNKS - 1, square_send, square_recv)
    split_right(square, 2, half_cols, half_cols)
    for chunk in range(CHUNKS // 2, CHUNKS):
        wait_next(square, chunk, square_send, square_recv)
    split_right(square, 1, half_cols, half_cols)
    accumulate([(1, 1), (2, 1)], True)

    for i in range(tile_rows):
        span = slice(i * tr, (i + 1) * tr)
        out_ref[span, :] = 3.0 * square[0, span, :] - 2.0 * masked_by_tiles(cube[span, :], i * tr)

    def all_sent(whole, send_sem):
        pltpu.make_async_copy(whole, whole, send_sem).wait()

    for section in range(SECTIONS):
        source = lax.rem(r + section, block_count)
        whole = left.at[section, half]

        @pl.when(jnp.logical_and(has_prev, source >= place))
        def _():
            all_sent(whole, z_send.at[0, section])

        @pl.when(jnp.logical_and(has_next, source <= place))
        def _():
            all_sent(whole, z_send.at[1, section])

        all_sent(whole, y_send.at[section])
    for sems in (right_send, square_send):
        for k in range(2):
            all_sent(right.at[0], sems.at[k])


def per_device(density, occupancy):
    blk, half_cols = density.shape
    row_count, col_count = lax.axis_size("row"), lax.axis_size("col")
    dma = pltpu.SemaphoreType.DMA
    wide = (SECTIONS, 2, blk, half_cols)
    tall = (SECTIONS, blk, half_cols)
    flops = 12 * blk * SECTIONS * blk * half_cols
    return pl.pallas_call(
        functools.partial(kernel, row_count, col_count),
        out_shape=jax.ShapeDtypeStruct(density.shape, jnp.float32),
        in_specs=[
            pl.BlockSpec(memory_space=pltpu.SMEM),
            pl.BlockSpec(memory_space=pltpu.HBM),
        ],
        out_specs=pl.BlockSpec(memory_space=pltpu.VMEM),
        scratch_shapes=[
            pltpu.VMEM(wide, jnp.float32),
            pltpu.VMEM(wide, jnp.bfloat16),
            pltpu.VMEM(wide, jnp.bfloat16),
            pltpu.VMEM(tall, jnp.float32),
            pltpu.VMEM(tall, jnp.float32),
            pltpu.VMEM(tall, jnp.bfloat16),
            pltpu.VMEM(tall, jnp.bfloat16),
            pltpu.VMEM((blk, half_cols), jnp.float32),
            dma((SECTIONS, 2, CHUNKS)),
            dma((2, SECTIONS)),
            dma((SECTIONS,)),
            dma((2, CHUNKS)),
            dma((2,)),
            dma((2, CHUNKS)),
            dma((2,)),
            dma,
        ],
        compiler_params=pltpu.CompilerParams(
            collective_id=0, has_side_effects=True, vmem_limit_bytes=40 * 2**20
        ),
        cost_estimate=pl.CostEstimate(
            flops=flops, bytes_accessed=2 * 4 * blk * half_cols, transcendentals=0
        ),
    )(occupancy.T, density)


def solution(mesh):
    in_specs = (P("row", "col"), P("row", "col"))
    out_specs = P("row", "col")
    return jax.shard_map(
        per_device, mesh=mesh, in_specs=in_specs, out_specs=out_specs, check_vma=False
    )
```

```python
import functools

import jax
import jax.numpy as jnp
from jax import lax
from jax.experimental import pallas as pl
from jax.experimental.pallas import tpu as pltpu
from jax.sharding import PartitionSpec as P

SECTIONS = 3
CHUNKS = 8
GROUPS = ((0, 2), (2, 2), (4, 2), (6, 1), (7, 1))
AHEAD = 2
ACROSS = 3
ROW_TILE = 128
MESH = pl.DeviceIdType.MESH


def split(values):
    high = values.astype(jnp.bfloat16)
    low = (values - high.astype(jnp.float32)).astype(jnp.bfloat16)
    return high, low


def product(left_high, left_low, right_high, right_low):
    dot = functools.partial(jnp.dot, preferred_element_type=jnp.float32)
    count = left_high.shape[0]
    both = dot(jnp.concatenate([left_high, left_low], axis=0), right_high)
    return both[:count] + (both[count:] + dot(left_high, right_low))


def kernel(
    row_count, col_count, occ_ref, den_ref, out_ref,
    left, left_high, left_low, right, square, right_high, right_low, cube,
    left_recv, z_send, y_send, right_recv, right_send, square_recv, square_send, load_sem, across_send,
):
    blk, half_cols = den_ref.shape
    rows = blk // CHUNKS
    tile_cols, tile_rows = occ_ref.shape
    tr, tc = blk // tile_rows, half_cols // tile_cols
    block_count = col_count // 2

    r, c = lax.axis_index("row"), lax.axis_index("col")
    place, half = lax.div(c, 2), lax.rem(c, 2)
    other = 1 - half
    core = lax.rem(r, 2)
    partner = c + 1 - 2 * half
    buddy = r + 1 - 2 * core
    above = lax.rem(r + row_count - 2, row_count)
    below = lax.rem(r + 2, row_count)
    has_prev, has_next = place > 0, place < block_count - 1
    own_section = lax.rem(place - r + block_count, block_count)

    load = pltpu.make_async_copy(den_ref, cube, load_sem)
    load.start()

    barrier = pltpu.get_barrier_semaphore()

    def greet(**device):
        pl.semaphore_signal(barrier, inc=1, device_id=device, device_id_type=MESH)

    @pl.when(has_prev)
    def _():
        greet(col=c - 2)

    @pl.when(has_next)
    def _():
        greet(col=c + 2)

    greet(col=partner)
    greet(row=buddy)
    greet(row=above)
    if row_count > 4:
        greet(row=below)

    def masked_by_tiles(values, first_row):
        count = min(tr, values.shape[0])
        lines = []
        for i in range(0, values.shape[0], count):
            line = []
            for k in range(tile_cols):
                weight = occ_ref[k, (first_row + i) // tr].astype(jnp.float32)
                line.append(values[i : i + count, k * tc : (k + 1) * tc] * weight)
            lines.append(jnp.concatenate(line, axis=1))
        return jnp.concatenate(lines, axis=0)

    load.wait()
    for i in range(tile_rows):
        part = masked_by_tiles(cube[i * tr : (i + 1) * tr, :], i * tr)
        right[0, i * tr : (i + 1) * tr, :] = part

        @pl.when(own_section < SECTIONS)
        def _():
            left[own_section, half, i * tr : (i + 1) * tr, :] = part

    pl.semaphore_wait(
        barrier,
        has_prev.astype(jnp.int32) + has_next.astype(jnp.int32) + (4 if row_count > 4 else 3),
    )

    def left_copy(section, side, chunk, send_sem, **device):
        piece = left.at[section, side, pl.ds(chunk * rows, rows), :]
        return pltpu.make_async_remote_copy(
            src_ref=piece, dst_ref=piece, send_sem=send_sem,
            recv_sem=left_recv.at[section, side, chunk],
            device_id=device, device_id_type=MESH,
        )

    def spread(section, chunk, to_prev, to_next):
        if to_prev:
            @pl.when(has_prev)
            def _():
                left_copy(section, half, chunk, z_send.at[0, section], col=c - 2).start()

        if to_next:
            @pl.when(has_next)
            def _():
                left_copy(section, half, chunk, z_send.at[1, section], col=c + 2).start()

        @pl.when(jnp.logical_or(section == own_section, chunk != ACROSS))
        def _():
            left_copy(section, half, chunk, y_send.at[section], col=partner).start()

    def pass_across(section, to_prev, to_next):
        wait_left(section, other, ACROSS)
        if to_prev:
            @pl.when(has_prev)
            def _():
                left_copy(section, other, ACROSS, across_send.at[0, section], col=c - 2).start()

        if to_next:
            @pl.when(has_next)
            def _():
                left_copy(section, other, ACROSS, across_send.at[1, section], col=c + 2).start()

    def wait_left(section, side, chunk):
        left_copy(section, side, chunk, y_send.at[section], col=partner).wait_recv()

    def send_own(chunk):
        @pl.when(own_section < SECTIONS)
        def _():
            spread(own_section, chunk, True, True)

    def forward(now):
        if now + AHEAD < CHUNKS:
            send_own(now + AHEAD)

        def step(distance, carry):
            chunk = now + 1 - distance
            for sign in (-1, 1):
                source = place + sign * distance
                section = lax.rem(source - r + 2 * block_count, block_count)
                inside = source >= 0 if sign < 0 else source < block_count

                @pl.when(jnp.logical_and(inside, section < SECTIONS))
                def _():
                    wait_left(section, half, chunk)
                    spread(section, chunk, sign > 0, sign < 0)

            return carry

        def step_across(distance):
            if distance == 0:
                @pl.when(own_section < SECTIONS)
                def _():
                    pass_across(own_section, True, True)

                return
            for sign in (-1, 1):
                source = place + sign * distance
                section = lax.rem(source - r + 2 * block_count, block_count)
                inside = source >= 0 if sign < 0 else source < block_count

                @pl.when(jnp.logical_and(inside, section < SECTIONS))
                def _():
                    pass_across(section, sign > 0, sign < 0)

        lax.fori_loop(max(1, now + 2 - CHUNKS), min(block_count - 1, now + 1) + 1, step, 0)
        if 0 <= now - ACROSS < block_count:
            step_across(now - ACROSS)

    def right_copy(buffer, from_slot, to_slot, chunk, send_sem, recv_sems, device_row):
        span = pl.ds(chunk * rows, rows)
        return pltpu.make_async_remote_copy(
            src_ref=buffer.at[from_slot, span, :], dst_ref=buffer.at[to_slot, span, :],
            send_sem=send_sem, recv_sem=recv_sems.at[to_slot - 1, chunk],
            device_id={"row": device_row}, device_id_type=MESH,
        )

    def send_right(buffer, chunk, send_sems, recv_sems):
        right_copy(buffer, 0, 2, chunk, send_sems.at[0], recv_sems, above).start()

        @pl.when(core == 1)
        def _():
            right_copy(buffer, 0, 1, chunk, send_sems.at[1], recv_sems, buddy).start()

    def relay_right(buffer, chunk, send_sems, recv_sems):
        right_copy(buffer, 0, 2, chunk, send_sems.at[0], recv_sems, above).wait_recv()

        @pl.when(core == 0)
        def _():
            right_copy(buffer, 2, 1, chunk, send_sems.at[1], recv_sems, buddy).start()

    def wait_next(buffer, chunk, send_sems, recv_sems):
        right_copy(buffer, 0, 1, chunk, send_sems.at[1], recv_sems, buddy).wait_recv()

    def split_right(buffer, slot, first, count):
        high, low = split(buffer[slot, first : first + count, :])
        right_high[slot, first : first + count, :] = high
        right_low[slot, first : first + count, :] = low

    def consume(first, count):
        span = slice(first * rows, (first + count) * rows)
        for chunk in range(first, first + count):
            for section in range(SECTIONS if chunk != ACROSS else 0):
                wait_left(section, other, chunk)
        total = jnp.zeros((count * rows, half_cols), jnp.float32)
        for section in range(SECTIONS):
            for side in range(2):
                high, low = split(left[section, side, span, :])
                left_high[section, side, span, :] = high
                left_low[section, side, span, :] = low
                depth = slice(side * half_cols, (side + 1) * half_cols)
                total = total + product(
                    high, low, right_high[section, depth, :], right_low[section, depth, :]
                )
        square[0, span, :] = masked_by_tiles(total, first * rows)
        for chunk in range(first, first + count):
            send_right(square, chunk, square_send, square_recv)

    for chunk in range(CHUNKS):
        send_right(right, chunk, right_send, right_recv)
    for chunk in range(AHEAD):
        send_own(chunk)

    lag = block_count - 1
    pending = None
    for now in range(CHUNKS + lag):
        if now < CHUNKS + lag - 1:
            forward(now)
        done = [g for g in GROUPS if g[0] + g[1] - 1 + lag == now]
        if not done:
            continue
        if done[0][0] == 0:
            for chunk in range(CHUNKS):
                relay_right(right, chunk, right_send, right_recv)
            split_right(right, 0, 0, blk)
            split_right(right, 2, 0, blk)
            for chunk in range(CHUNKS):
                wait_next(right, chunk, right_send, right_recv)
            split_right(right, 1, 0, blk)
        consume(*done[0])
        if pending:
            for chunk in range(pending[0], sum(pending)):
                relay_right(square, chunk, square_send, square_recv)
        pending = done[0]

    def accumulate(terms, last):
        def step(tile, carry):
            span = pl.ds(pl.multiple_of(tile * ROW_TILE, ROW_TILE), ROW_TILE)
            total = cube[span, :] if last else jnp.zeros((ROW_TILE, half_cols), jnp.float32)
            for section, side in terms:
                depth = slice(side * half_cols, (side + 1) * half_cols)
                total = total + product(
                    left_high[section, side, span, :], left_low[section, side, span, :],
                    right_high[section, depth, :], right_low[section, depth, :],
                )
            cube[span, :] = total
            return carry

        lax.fori_loop(0, blk // ROW_TILE, step, 0)

    split_right(square, 0, 0, blk)
    for chunk in range(CHUNKS // 2):
        wait_next(square, chunk, square_send, square_recv)
    split_right(square, 1, 0, half_cols)
    split_right(square, 2, 0, half_cols)
    accumulate([(0, 0), (0, 1), (1, 0), (2, 0)], False)
    relay_right(square, CHUNKS - 1, square_send, square_recv)
    split_right(square, 2, half_cols, half_cols)
    for chunk in range(CHUNKS // 2, CHUNKS):
        wait_next(square, chunk, square_send, square_recv)
    split_right(square, 1, half_cols, half_cols)
    accumulate([(1, 1), (2, 1)], True)

    for i in range(tile_rows):
        span = slice(i * tr, (i + 1) * tr)
        out_ref[span, :] = 3.0 * square[0, span, :] - 2.0 * masked_by_tiles(cube[span, :], i * tr)

    def all_sent(whole, send_sem):
        pltpu.make_async_copy(whole, whole, send_sem).wait()

    for section in range(SECTIONS):
        source = lax.rem(r + section, block_count)
        whole = left.at[section, half]
        piece = left.at[section, other, pl.ds(0, rows), :]

        @pl.when(jnp.logical_and(has_prev, source >= place))
        def _():
            all_sent(whole, z_send.at[0, section])
            all_sent(piece, across_send.at[0, section])

        @pl.when(jnp.logical_and(has_next, source <= place))
        def _():
            all_sent(whole, z_send.at[1, section])
            all_sent(piece, across_send.at[1, section])

        all_sent(left.at[section, half, pl.ds(0, blk - rows), :], y_send.at[section])

        @pl.when(source == place)
        def _():
            all_sent(piece, y_send.at[section])

    for sems in (right_send, square_send):
        for k in range(2):
            all_sent(right.at[0], sems.at[k])


def per_device(density, occupancy):
    blk, half_cols = density.shape
    row_count, col_count = lax.axis_size("row"), lax.axis_size("col")
    dma = pltpu.SemaphoreType.DMA
    wide = (SECTIONS, 2, blk, half_cols)
    tall = (SECTIONS, blk, half_cols)
    flops = 12 * blk * SECTIONS * blk * half_cols
    return pl.pallas_call(
        functools.partial(kernel, row_count, col_count),
        out_shape=jax.ShapeDtypeStruct(density.shape, jnp.float32),
        in_specs=[
            pl.BlockSpec(memory_space=pltpu.SMEM),
            pl.BlockSpec(memory_space=pltpu.HBM),
        ],
        out_specs=pl.BlockSpec(memory_space=pltpu.VMEM),
        scratch_shapes=[
            pltpu.VMEM(wide, jnp.float32),
            pltpu.VMEM(wide, jnp.bfloat16),
            pltpu.VMEM(wide, jnp.bfloat16),
            pltpu.VMEM(tall, jnp.float32),
            pltpu.VMEM(tall, jnp.float32),
            pltpu.VMEM(tall, jnp.bfloat16),
            pltpu.VMEM(tall, jnp.bfloat16),
            pltpu.VMEM((blk, half_cols), jnp.float32),
            dma((SECTIONS, 2, CHUNKS)),
            dma((2, SECTIONS)),
            dma((SECTIONS,)),
            dma((2, CHUNKS)),
            dma((2,)),
            dma((2, CHUNKS)),
            dma((2,)),
            dma,
            dma((2, SECTIONS)),
        ],
        compiler_params=pltpu.CompilerParams(
            collective_id=0, has_side_effects=True, vmem_limit_bytes=64 * 2**20 - 800 * 2**10
        ),
        cost_estimate=pl.CostEstimate(
            flops=flops, bytes_accessed=2 * 4 * blk * half_cols, transcendentals=0
        ),
    )(occupancy.T, density)


def solution(mesh):
    in_specs = (P("row", "col"), P("row", "col"))
    out_specs = P("row", "col")
    return jax.shard_map(
        per_device, mesh=mesh, in_specs=in_specs, out_specs=out_specs, check_vma=False
    )
```

```python
import functools

import jax
import jax.numpy as jnp
from jax import lax
from jax.experimental import pallas as pl
from jax.experimental.pallas import tpu as pltpu
from jax.sharding import PartitionSpec as P

SECTIONS = 3
CHUNKS = 8
GROUPS = ((0, 2), (2, 2), (4, 2), (6, 1), (7, 1))
AHEAD = 2
ROW_TILE = 128
MESH = pl.DeviceIdType.MESH


def split(values):
    high = values.astype(jnp.bfloat16)
    low = (values - high.astype(jnp.float32)).astype(jnp.bfloat16)
    return high, low


def product(left_high, left_low, right_high, right_low):
    dot = functools.partial(jnp.dot, preferred_element_type=jnp.float32)
    count = left_high.shape[0]
    both = dot(jnp.concatenate([left_high, left_low], axis=0), right_high)
    return both[:count] + (both[count:] + dot(left_high, right_low))


def kernel(
    row_count, col_count, occ_ref, den_ref, out_ref,
    left, left_high, left_low, right, square, right_high, right_low, cube,
    left_recv, z_send, y_send, right_recv, right_send, square_recv, square_send, load_sem,
):
    blk, half_cols = den_ref.shape
    rows = blk // CHUNKS
    tile_cols, tile_rows = occ_ref.shape
    tr, tc = blk // tile_rows, half_cols // tile_cols
    block_count = col_count // 2

    r, c = lax.axis_index("row"), lax.axis_index("col")
    place, half = lax.div(c, 2), lax.rem(c, 2)
    other = 1 - half
    core = lax.rem(r, 2)
    partner = c + 1 - 2 * half
    buddy = r + 1 - 2 * core
    above = lax.rem(r + row_count - 2, row_count)
    below = lax.rem(r + 2, row_count)
    own_section = lax.rem(place - r + block_count, block_count)

    load = pltpu.make_async_copy(den_ref, cube, load_sem)
    load.start()

    barrier = pltpu.get_barrier_semaphore()

    def greet(**device):
        pl.semaphore_signal(barrier, inc=1, device_id=device, device_id_type=MESH)

    def greet_line(distance, carry):
        @pl.when(place >= distance)
        def _():
            greet(col=c - 2 * distance)

        @pl.when(place + distance < block_count)
        def _():
            greet(col=c + 2 * distance)

        return carry

    lax.fori_loop(1, block_count, greet_line, 0)
    greet(col=partner)
    greet(row=buddy)
    greet(row=above)
    if row_count > 4:
        greet(row=below)

    def masked_by_tiles(values, first_row):
        count = min(tr, values.shape[0])
        lines = []
        for i in range(0, values.shape[0], count):
            line = []
            for k in range(tile_cols):
                weight = occ_ref[k, (first_row + i) // tr].astype(jnp.float32)
                line.append(values[i : i + count, k * tc : (k + 1) * tc] * weight)
            lines.append(jnp.concatenate(line, axis=1))
        return jnp.concatenate(lines, axis=0)

    load.wait()
    for i in range(tile_rows):
        part = masked_by_tiles(cube[i * tr : (i + 1) * tr, :], i * tr)
        right[0, i * tr : (i + 1) * tr, :] = part

        @pl.when(own_section < SECTIONS)
        def _():
            left[own_section, half, i * tr : (i + 1) * tr, :] = part

    pl.semaphore_wait(barrier, block_count - 1 + (4 if row_count > 4 else 3))

    def left_copy(section, side, chunk, send_sem, **device):
        piece = left.at[section, side, pl.ds(chunk * rows, rows), :]
        return pltpu.make_async_remote_copy(
            src_ref=piece, dst_ref=piece, send_sem=send_sem,
            recv_sem=left_recv.at[section, side, chunk],
            device_id=device, device_id_type=MESH,
        )

    def to_partner(section, chunk):
        left_copy(section, half, chunk, y_send.at[section], col=partner).start()

    def wait_left(section, side, chunk):
        left_copy(section, side, chunk, y_send.at[section], col=partner).wait_recv()

    def send_own(chunk):
        @pl.when(own_section < SECTIONS)
        def _():
            def step(distance, carry):
                @pl.when(place >= distance)
                def _():
                    left_copy(
                        own_section, half, chunk, z_send.at[0, distance - 1], col=c - 2 * distance
                    ).start()

                @pl.when(place + distance < block_count)
                def _():
                    left_copy(
                        own_section, half, chunk, z_send.at[1, distance - 1], col=c + 2 * distance
                    ).start()

                return carry

            to_partner(own_section, chunk)
            lax.fori_loop(1, block_count, step, 0)

    def forward(chunk):
        if chunk + AHEAD < CHUNKS:
            send_own(chunk + AHEAD)
        for section in range(SECTIONS):
            @pl.when(section != own_section)
            def _():
                wait_left(section, half, chunk)
                to_partner(section, chunk)

    def right_copy(buffer, from_slot, to_slot, chunk, send_sem, recv_sems, device_row):
        span = pl.ds(chunk * rows, rows)
        return pltpu.make_async_remote_copy(
            src_ref=buffer.at[from_slot, span, :], dst_ref=buffer.at[to_slot, span, :],
            send_sem=send_sem, recv_sem=recv_sems.at[to_slot - 1, chunk],
            device_id={"row": device_row}, device_id_type=MESH,
        )

    def send_right(buffer, chunk, send_sems, recv_sems):
        right_copy(buffer, 0, 2, chunk, send_sems.at[0], recv_sems, above).start()

        @pl.when(core == 1)
        def _():
            right_copy(buffer, 0, 1, chunk, send_sems.at[1], recv_sems, buddy).start()

    def relay_right(buffer, chunk, send_sems, recv_sems):
        right_copy(buffer, 0, 2, chunk, send_sems.at[0], recv_sems, above).wait_recv()

        @pl.when(core == 0)
        def _():
            right_copy(buffer, 2, 1, chunk, send_sems.at[1], recv_sems, buddy).start()

    def wait_next(buffer, chunk, send_sems, recv_sems):
        right_copy(buffer, 0, 1, chunk, send_sems.at[1], recv_sems, buddy).wait_recv()

    def split_right(buffer, slot, first, count):
        high, low = split(buffer[slot, first : first + count, :])
        right_high[slot, first : first + count, :] = high
        right_low[slot, first : first + count, :] = low

    def consume(first, count):
        span = slice(first * rows, (first + count) * rows)
        for chunk in range(first, first + count):
            for section in range(SECTIONS):
                wait_left(section, other, chunk)
        total = jnp.zeros((count * rows, half_cols), jnp.float32)
        for section in range(SECTIONS):
            for side in range(2):
                high, low = split(left[section, side, span, :])
                left_high[section, side, span, :] = high
                left_low[section, side, span, :] = low
                depth = slice(side * half_cols, (side + 1) * half_cols)
                total = total + product(
                    high, low, right_high[section, depth, :], right_low[section, depth, :]
                )
        square[0, span, :] = masked_by_tiles(total, first * rows)
        for chunk in range(first, first + count):
            send_right(square, chunk, square_send, square_recv)

    for chunk in range(CHUNKS):
        send_right(right, chunk, right_send, right_recv)
    for chunk in range(AHEAD):
        send_own(chunk)

    lag = 1
    pending = None
    for now in range(CHUNKS + lag):
        if now < CHUNKS:
            forward(now)
        done = [g for g in GROUPS if g[0] + g[1] - 1 + lag == now]
        if not done:
            continue
        if done[0][0] == 0:
            for chunk in range(CHUNKS):
                relay_right(right, chunk, right_send, right_recv)
            split_right(right, 0, 0, blk)
            split_right(right, 2, 0, blk)
            for chunk in range(CHUNKS):
                wait_next(right, chunk, right_send, right_recv)
            split_right(right, 1, 0, blk)
        consume(*done[0])
        if pending:
            for chunk in range(pending[0], sum(pending)):
                relay_right(square, chunk, square_send, square_recv)
        pending = done[0]

    def accumulate(terms, last):
        def step(tile, carry):
            span = pl.ds(pl.multiple_of(tile * ROW_TILE, ROW_TILE), ROW_TILE)
            total = cube[span, :] if last else jnp.zeros((ROW_TILE, half_cols), jnp.float32)
            for section, side in terms:
                depth = slice(side * half_cols, (side + 1) * half_cols)
                total = total + product(
                    left_high[section, side, span, :], left_low[section, side, span, :],
                    right_high[section, depth, :], right_low[section, depth, :],
                )
            cube[span, :] = total
            return carry

        lax.fori_loop(0, blk // ROW_TILE, step, 0)

    split_right(square, 0, 0, blk)
    for chunk in range(CHUNKS // 2):
        wait_next(square, chunk, square_send, square_recv)
    split_right(square, 1, 0, half_cols)
    split_right(square, 2, 0, half_cols)
    accumulate([(0, 0), (0, 1), (1, 0), (2, 0)], False)
    relay_right(square, CHUNKS - 1, square_send, square_recv)
    split_right(square, 2, half_cols, half_cols)
    for chunk in range(CHUNKS // 2, CHUNKS):
        wait_next(square, chunk, square_send, square_recv)
    split_right(square, 1, half_cols, half_cols)
    accumulate([(1, 1), (2, 1)], True)

    for i in range(tile_rows):
        span = slice(i * tr, (i + 1) * tr)
        out_ref[span, :] = 3.0 * square[0, span, :] - 2.0 * masked_by_tiles(cube[span, :], i * tr)

    def all_sent(whole, send_sem):
        pltpu.make_async_copy(whole, whole, send_sem).wait()

    for section in range(SECTIONS):
        all_sent(left.at[section, half], y_send.at[section])

    @pl.when(own_section < SECTIONS)
    def _():
        def step(distance, carry):
            @pl.when(place >= distance)
            def _():
                all_sent(left.at[own_section, half], z_send.at[0, distance - 1])

            @pl.when(place + distance < block_count)
            def _():
                all_sent(left.at[own_section, half], z_send.at[1, distance - 1])

            return carry

        lax.fori_loop(1, block_count, step, 0)

    for sems in (right_send, square_send):
        for k in range(2):
            all_sent(right.at[0], sems.at[k])


def per_device(density, occupancy):
    blk, half_cols = density.shape
    row_count, col_count = lax.axis_size("row"), lax.axis_size("col")
    dma = pltpu.SemaphoreType.DMA
    wide = (SECTIONS, 2, blk, half_cols)
    tall = (SECTIONS, blk, half_cols)
    flops = 12 * blk * SECTIONS * blk * half_cols
    return pl.pallas_call(
        functools.partial(kernel, row_count, col_count),
        out_shape=jax.ShapeDtypeStruct(density.shape, jnp.float32),
        in_specs=[
            pl.BlockSpec(memory_space=pltpu.SMEM),
            pl.BlockSpec(memory_space=pltpu.HBM),
        ],
        out_specs=pl.BlockSpec(memory_space=pltpu.VMEM),
        scratch_shapes=[
            pltpu.VMEM(wide, jnp.float32),
            pltpu.VMEM(wide, jnp.bfloat16),
            pltpu.VMEM(wide, jnp.bfloat16),
            pltpu.VMEM(tall, jnp.float32),
            pltpu.VMEM(tall, jnp.float32),
            pltpu.VMEM(tall, jnp.bfloat16),
            pltpu.VMEM(tall, jnp.bfloat16),
            pltpu.VMEM((blk, half_cols), jnp.float32),
            dma((SECTIONS, 2, CHUNKS)),
            dma((2, col_count // 2 - 1)),
            dma((SECTIONS,)),
            dma((2, CHUNKS)),
            dma((2,)),
            dma((2, CHUNKS)),
            dma((2,)),
            dma,
        ],
        compiler_params=pltpu.CompilerParams(
            collective_id=0, has_side_effects=True, vmem_limit_bytes=40 * 2**20
        ),
        cost_estimate=pl.CostEstimate(
            flops=flops, bytes_accessed=2 * 4 * blk * half_cols, transcendentals=0
        ),
    )(occupancy.T, density)


def solution(mesh):
    in_specs = (P("row", "col"), P("row", "col"))
    out_specs = P("row", "col")
    return jax.shard_map(
        per_device, mesh=mesh, in_specs=in_specs, out_specs=out_specs, check_vma=False
    )
```

```python
import functools

import jax
import jax.numpy as jnp
from jax import lax
from jax.experimental import pallas as pl
from jax.experimental.pallas import tpu as pltpu
from jax.sharding import PartitionSpec as P

SECTIONS = 3
CHUNKS = 8
GROUPS = ((0, 2), (2, 2), (4, 2), (6, 1), (7, 1))
AHEAD = 4
ROW_TILE = 128
MESH = pl.DeviceIdType.MESH


def split(values):
    high = values.astype(jnp.bfloat16)
    low = (values - high.astype(jnp.float32)).astype(jnp.bfloat16)
    return high, low


def product(left_high, left_low, right_high, right_low):
    dot = functools.partial(jnp.dot, preferred_element_type=jnp.float32)
    count = left_high.shape[0]
    both = dot(jnp.concatenate([left_high, left_low], axis=0), right_high)
    return both[:count] + (both[count:] + dot(left_high, right_low))


def kernel(
    row_count, col_count, occ_ref, den_ref, out_ref,
    left, left_high, left_low, right, square, right_high, right_low, cube,
    left_recv, z_send, y_send, right_recv, right_send, square_recv, square_send, load_sem,
):
    blk, half_cols = den_ref.shape
    rows = blk // CHUNKS
    tile_cols, tile_rows = occ_ref.shape
    tr, tc = blk // tile_rows, half_cols // tile_cols
    block_count = col_count // 2

    r, c = lax.axis_index("row"), lax.axis_index("col")
    place, half = lax.div(c, 2), lax.rem(c, 2)
    other = 1 - half
    core = lax.rem(r, 2)
    partner = c + 1 - 2 * half
    buddy = r + 1 - 2 * core
    above = lax.rem(r + row_count - 2, row_count)
    below = lax.rem(r + 2, row_count)
    has_prev, has_next = place > 0, place < block_count - 1
    own_section = lax.rem(place - r + block_count, block_count)

    load = pltpu.make_async_copy(den_ref, cube, load_sem)
    load.start()

    barrier = pltpu.get_barrier_semaphore()

    def greet(**device):
        pl.semaphore_signal(barrier, inc=1, device_id=device, device_id_type=MESH)

    @pl.when(has_prev)
    def _():
        greet(col=c - 2)

    @pl.when(has_next)
    def _():
        greet(col=c + 2)

    greet(col=partner)
    greet(row=buddy)
    greet(row=above)
    if row_count > 4:
        greet(row=below)

    def masked_by_tiles(values, first_row):
        count = min(tr, values.shape[0])
        lines = []
        for i in range(0, values.shape[0], count):
            line = []
            for k in range(tile_cols):
                weight = occ_ref[k, (first_row + i) // tr].astype(jnp.float32)
                line.append(values[i : i + count, k * tc : (k + 1) * tc] * weight)
            lines.append(jnp.concatenate(line, axis=1))
        return jnp.concatenate(lines, axis=0)

    load.wait()
    for i in range(tile_rows):
        part = masked_by_tiles(cube[i * tr : (i + 1) * tr, :], i * tr)
        right[0, i * tr : (i + 1) * tr, :] = part

        @pl.when(own_section < SECTIONS)
        def _():
            left[own_section, half, i * tr : (i + 1) * tr, :] = part

    pl.semaphore_wait(
        barrier,
        has_prev.astype(jnp.int32) + has_next.astype(jnp.int32) + (4 if row_count > 4 else 3),
    )

    def left_copy(section, side, chunk, send_sem, **device):
        piece = left.at[section, side, pl.ds(chunk * rows, rows), :]
        return pltpu.make_async_remote_copy(
            src_ref=piece, dst_ref=piece, send_sem=send_sem,
            recv_sem=left_recv.at[section, side, chunk],
            device_id=device, device_id_type=MESH,
        )

    def spread(section, chunk, to_prev, to_next):
        if to_prev:
            @pl.when(has_prev)
            def _():
                left_copy(section, half, chunk, z_send.at[0, section], col=c - 2).start()

        if to_next:
            @pl.when(has_next)
            def _():
                left_copy(section, half, chunk, z_send.at[1, section], col=c + 2).start()

        left_copy(section, half, chunk, y_send.at[section], col=partner).start()

    def wait_left(section, side, chunk):
        left_copy(section, side, chunk, y_send.at[section], col=partner).wait_recv()

    def send_own(chunk):
        @pl.when(own_section < SECTIONS)
        def _():
            spread(own_section, chunk, True, True)

    def forward(now):
        if now + AHEAD < CHUNKS:
            send_own(now + AHEAD)

        def step(distance, carry):
            chunk = now + 1 - distance
            for sign in (-1, 1):
                source = place + sign * distance
                section = lax.rem(source - r + 2 * block_count, block_count)
                inside = source >= 0 if sign < 0 else source < block_count

                @pl.when(jnp.logical_and(inside, section < SECTIONS))
                def _():
                    wait_left(section, half, chunk)
                    spread(section, chunk, sign > 0, sign < 0)

            return carry

        lax.fori_loop(max(1, now + 2 - CHUNKS), min(block_count - 1, now + 1) + 1, step, 0)

    def right_copy(buffer, from_slot, to_slot, chunk, send_sem, recv_sems, device_row):
        span = pl.ds(chunk * rows, rows)
        return pltpu.make_async_remote_copy(
            src_ref=buffer.at[from_slot, span, :], dst_ref=buffer.at[to_slot, span, :],
            send_sem=send_sem, recv_sem=recv_sems.at[to_slot - 1, chunk],
            device_id={"row": device_row}, device_id_type=MESH,
        )

    def send_right(buffer, chunk, send_sems, recv_sems):
        right_copy(buffer, 0, 2, chunk, send_sems.at[0], recv_sems, above).start()

        @pl.when(core == 1)
        def _():
            right_copy(buffer, 0, 1, chunk, send_sems.at[1], recv_sems, buddy).start()

    def relay_right(buffer, chunk, send_sems, recv_sems):
        right_copy(buffer, 0, 2, chunk, send_sems.at[0], recv_sems, above).wait_recv()

        @pl.when(core == 0)
        def _():
            right_copy(buffer, 2, 1, chunk, send_sems.at[1], recv_sems, buddy).start()

    def wait_next(buffer, chunk, send_sems, recv_sems):
        right_copy(buffer, 0, 1, chunk, send_sems.at[1], recv_sems, buddy).wait_recv()

    def split_right(buffer, slot, first, count):
        high, low = split(buffer[slot, first : first + count, :])
        right_high[slot, first : first + count, :] = high
        right_low[slot, first : first + count, :] = low

    def consume(first, count):
        span = slice(first * rows, (first + count) * rows)
        for chunk in range(first, first + count):
            for section in range(SECTIONS):
                wait_left(section, other, chunk)
        total = jnp.zeros((count * rows, half_cols), jnp.float32)
        for section in range(SECTIONS):
            for side in range(2):
                high, low = split(left[section, side, span, :])
                left_high[section, side, span, :] = high
                left_low[section, side, span, :] = low
                depth = slice(side * half_cols, (side + 1) * half_cols)
                total = total + product(
                    high, low, right_high[section, depth, :], right_low[section, depth, :]
                )
        square[0, span, :] = masked_by_tiles(total, first * rows)
        for chunk in range(first, first + count):
            send_right(square, chunk, square_send, square_recv)

    for chunk in range(CHUNKS):
        send_right(right, chunk, right_send, right_recv)
    for chunk in range(AHEAD):
        send_own(chunk)

    lag = block_count - 1
    pending = None
    for now in range(CHUNKS + lag):
        if now < CHUNKS + lag - 1:
            forward(now)
        done = [g for g in GROUPS if g[0] + g[1] - 1 + lag == now]
        if not done:
            continue
        if done[0][0] == 0:
            for chunk in range(CHUNKS):
                relay_right(right, chunk, right_send, right_recv)
            split_right(right, 0, 0, blk)
            split_right(right, 2, 0, blk)
            for chunk in range(CHUNKS):
                wait_next(right, chunk, right_send, right_recv)
            split_right(right, 1, 0, blk)
        consume(*done[0])
        if pending:
            for chunk in range(pending[0], sum(pending)):
                relay_right(square, chunk, square_send, square_recv)
        pending = done[0]

    def accumulate(terms, last):
        def step(tile, carry):
            span = pl.ds(pl.multiple_of(tile * ROW_TILE, ROW_TILE), ROW_TILE)
            total = cube[span, :] if last else jnp.zeros((ROW_TILE, half_cols), jnp.float32)
            for section, first, end in terms:
                side = first // half_cols
                depth = slice(first, end)
                cols = slice(first - side * half_cols, end - side * half_cols)
                total = total + product(
                    left_high[section, side, span, cols], left_low[section, side, span, cols],
                    right_high[section, depth, :], right_low[section, depth, :],
                )
            cube[span, :] = total
            return carry

        lax.fori_loop(0, blk // ROW_TILE, step, 0)

    late = blk - half_cols // 2
    split_right(square, 0, 0, blk)
    for chunk in range(late // rows):
        wait_next(square, chunk, square_send, square_recv)
    split_right(square, 1, 0, late)
    split_right(square, 2, 0, late)
    early = [(0, 0, half_cols), (0, half_cols, blk)]
    for section in range(1, SECTIONS):
        early += [(section, 0, half_cols), (section, half_cols, late)]
    accumulate(early, False)
    relay_right(square, CHUNKS - 1, square_send, square_recv)
    split_right(square, 2, late, blk - late)
    for chunk in range(late // rows, CHUNKS):
        wait_next(square, chunk, square_send, square_recv)
    split_right(square, 1, late, blk - late)
    accumulate([(section, late, blk) for section in range(1, SECTIONS)], True)

    for i in range(tile_rows):
        span = slice(i * tr, (i + 1) * tr)
        out_ref[span, :] = 3.0 * square[0, span, :] - 2.0 * masked_by_tiles(cube[span, :], i * tr)

    def all_sent(whole, send_sem):
        pltpu.make_async_copy(whole, whole, send_sem).wait()

    for section in range(SECTIONS):
        source = lax.rem(r + section, block_count)
        whole = left.at[section, half]

        @pl.when(jnp.logical_and(has_prev, source >= place))
        def _():
            all_sent(whole, z_send.at[0, section])

        @pl.when(jnp.logical_and(has_next, source <= place))
        def _():
            all_sent(whole, z_send.at[1, section])

        all_sent(whole, y_send.at[section])
    for sems in (right_send, square_send):
        for k in range(2):
            all_sent(right.at[0], sems.at[k])


def per_device(density, occupancy):
    blk, half_cols = density.shape
    row_count, col_count = lax.axis_size("row"), lax.axis_size("col")
    dma = pltpu.SemaphoreType.DMA
    wide = (SECTIONS, 2, blk, half_cols)
    tall = (SECTIONS, blk, half_cols)
    flops = 12 * blk * SECTIONS * blk * half_cols
    return pl.pallas_call(
        functools.partial(kernel, row_count, col_count),
        out_shape=jax.ShapeDtypeStruct(density.shape, jnp.float32),
        in_specs=[
            pl.BlockSpec(memory_space=pltpu.SMEM),
            pl.BlockSpec(memory_space=pltpu.HBM),
        ],
        out_specs=pl.BlockSpec(memory_space=pltpu.VMEM),
        scratch_shapes=[
            pltpu.VMEM(wide, jnp.float32),
            pltpu.VMEM(wide, jnp.bfloat16),
            pltpu.VMEM(wide, jnp.bfloat16),
            pltpu.VMEM(tall, jnp.float32),
            pltpu.VMEM(tall, jnp.float32),
            pltpu.VMEM(tall, jnp.bfloat16),
            pltpu.VMEM(tall, jnp.bfloat16),
            pltpu.VMEM((blk, half_cols), jnp.float32),
            dma((SECTIONS, 2, CHUNKS)),
            dma((2, SECTIONS)),
            dma((SECTIONS,)),
            dma((2, CHUNKS)),
            dma((2,)),
            dma((2, CHUNKS)),
            dma((2,)),
            dma,
        ],
        compiler_params=pltpu.CompilerParams(
            collective_id=0, has_side_effects=True, vmem_limit_bytes=40 * 2**20
        ),
        cost_estimate=pl.CostEstimate(
            flops=flops, bytes_accessed=2 * 4 * blk * half_cols, transcendentals=0
        ),
    )(occupancy.T, density)


def solution(mesh):
    in_specs = (P("row", "col"), P("row", "col"))
    out_specs = P("row", "col")
    return jax.shard_map(
        per_device, mesh=mesh, in_specs=in_specs, out_specs=out_specs, check_vma=False
    )
```

```python
import functools

import jax
import jax.numpy as jnp
from jax import lax
from jax.experimental import pallas as pl
from jax.experimental.pallas import tpu as pltpu
from jax.sharding import PartitionSpec as P

SECTIONS = 3
CHUNKS = 8
GROUPS = ((0, 2), (2, 2), (4, 2), (6, 1), (7, 1))
AHEAD = 2
ROW_TILE = 128
MESH = pl.DeviceIdType.MESH


def split(values):
    high = values.astype(jnp.bfloat16)
    low = (values - high.astype(jnp.float32)).astype(jnp.bfloat16)
    return high, low


def product(left_high, left_low, right_high, right_low):
    dot = functools.partial(jnp.dot, preferred_element_type=jnp.float32)
    count = left_high.shape[0]
    both = dot(jnp.concatenate([left_high, left_low], axis=0), right_high)
    return both[:count] + (both[count:] + dot(left_high, right_low))


def kernel(
    row_count, col_count, occ_ref, den_ref, out_ref,
    left, left_high, left_low, right, square, right_high, right_low, cube,
    left_recv, z_send, y_send, right_recv, right_send, square_recv, square_send, load_sem,
):
    blk, half_cols = den_ref.shape
    rows = blk // CHUNKS
    tile_cols, tile_rows = occ_ref.shape
    tr, tc = blk // tile_rows, half_cols // tile_cols
    block_count = col_count // 2

    r, c = lax.axis_index("row"), lax.axis_index("col")
    place, half = lax.div(c, 2), lax.rem(c, 2)
    other = 1 - half
    core = lax.rem(r, 2)
    partner = c + 1 - 2 * half
    buddy = r + 1 - 2 * core
    above = lax.rem(r + row_count - 2, row_count)
    below = lax.rem(r + 2, row_count)
    has_prev, has_next = place > 0, place < block_count - 1
    own_section = lax.rem(place - r + block_count, block_count)

    load = pltpu.make_async_copy(den_ref, cube, load_sem)
    load.start()

    barrier = pltpu.get_barrier_semaphore()

    def greet(**device):
        pl.semaphore_signal(barrier, inc=1, device_id=device, device_id_type=MESH)

    @pl.when(has_prev)
    def _():
        greet(col=c - 2)

    @pl.when(has_next)
    def _():
        greet(col=c + 2)

    greet(col=partner)
    greet(row=buddy)
    greet(row=above)
    if row_count > 4:
        greet(row=below)

    def masked_by_tiles(values, first_row):
        count = min(tr, values.shape[0])
        lines = []
        for i in range(0, values.shape[0], count):
            line = []
            for k in range(tile_cols):
                weight = occ_ref[k, (first_row + i) // tr].astype(jnp.float32)
                line.append(values[i : i + count, k * tc : (k + 1) * tc] * weight)
            lines.append(jnp.concatenate(line, axis=1))
        return jnp.concatenate(lines, axis=0)

    load.wait()
    for i in range(tile_rows):
        part = masked_by_tiles(cube[i * tr : (i + 1) * tr, :], i * tr)
        right[0, i * tr : (i + 1) * tr, :] = part

        @pl.when(own_section < SECTIONS)
        def _():
            left[own_section, half, i * tr : (i + 1) * tr, :] = part

    pl.semaphore_wait(
        barrier,
        has_prev.astype(jnp.int32) + has_next.astype(jnp.int32) + (4 if row_count > 4 else 3),
    )

    def left_copy(section, side, chunk, send_sem, **device):
        piece = left.at[section, side, pl.ds(chunk * rows, rows), :]
        return pltpu.make_async_remote_copy(
            src_ref=piece, dst_ref=piece, send_sem=send_sem,
            recv_sem=left_recv.at[section, side, chunk],
            device_id=device, device_id_type=MESH,
        )

    def spread(section, chunk, to_prev, to_next):
        if to_prev:
            @pl.when(has_prev)
            def _():
                left_copy(section, half, chunk, z_send.at[0, section], col=c - 2).start()

        if to_next:
            @pl.when(has_next)
            def _():
                left_copy(section, half, chunk, z_send.at[1, section], col=c + 2).start()

        left_copy(section, half, chunk, y_send.at[section], col=partner).start()

    def wait_left(section, side, chunk):
        left_copy(section, side, chunk, y_send.at[section], col=partner).wait_recv()

    def send_own(chunk):
        @pl.when(own_section < SECTIONS)
        def _():
            spread(own_section, chunk, True, True)

    def forward(now):
        if now + AHEAD < CHUNKS:
            send_own(now + AHEAD)

        def step(distance, carry):
            chunk = now + 1 - distance
            for sign in (-1, 1):
                source = place + sign * distance
                section = lax.rem(source - r + 2 * block_count, block_count)
                inside = source >= 0 if sign < 0 else source < block_count

                @pl.when(jnp.logical_and(inside, section < SECTIONS))
                def _():
                    wait_left(section, half, chunk)
                    spread(section, chunk, sign > 0, sign < 0)

            return carry

        lax.fori_loop(max(1, now + 2 - CHUNKS), min(block_count - 1, now + 1) + 1, step, 0)

    def right_copy(buffer, from_slot, to_slot, chunk, send_sem, recv_sems, device_row):
        span = pl.ds(chunk * rows, rows)
        return pltpu.make_async_remote_copy(
            src_ref=buffer.at[from_slot, span, :], dst_ref=buffer.at[to_slot, span, :],
            send_sem=send_sem, recv_sem=recv_sems.at[to_slot - 1, chunk],
            device_id={"row": device_row}, device_id_type=MESH,
        )

    def send_right(buffer, chunk, send_sems, recv_sems):
        right_copy(buffer, 0, 2, chunk, send_sems.at[0], recv_sems, above).start()

        @pl.when(core == 1)
        def _():
            right_copy(buffer, 0, 1, chunk, send_sems.at[1], recv_sems, buddy).start()

    def relay_right(buffer, chunk, send_sems, recv_sems):
        right_copy(buffer, 0, 2, chunk, send_sems.at[0], recv_sems, above).wait_recv()

        @pl.when(core == 0)
        def _():
            right_copy(buffer, 2, 1, chunk, send_sems.at[1], recv_sems, buddy).start()

    def wait_next(buffer, chunk, send_sems, recv_sems):
        right_copy(buffer, 0, 1, chunk, send_sems.at[1], recv_sems, buddy).wait_recv()

    def split_right(buffer, slot, first, count):
        high, low = split(buffer[slot, first : first + count, :])
        right_high[slot, first : first + count, :] = high
        right_low[slot, first : first + count, :] = low

    def consume(first, count):
        span = slice(first * rows, (first + count) * rows)
        for chunk in range(first, first + count):
            for section in range(SECTIONS):
                wait_left(section, other, chunk)
        total = jnp.zeros((count * rows, half_cols), jnp.float32)
        for section in range(SECTIONS):
            for side in range(2):
                high, low = split(left[section, side, span, :])
                left_high[section, side, span, :] = high
                left_low[section, side, span, :] = low
                depth = slice(side * half_cols, (side + 1) * half_cols)
                total = total + product(
                    high, low, right_high[section, depth, :], right_low[section, depth, :]
                )
        square[0, span, :] = masked_by_tiles(total, first * rows)
        for chunk in range(first, first + count):
            send_right(square, chunk, square_send, square_recv)

    for chunk in range(CHUNKS):
        send_right(right, chunk, right_send, right_recv)
    for chunk in range(AHEAD):
        send_own(chunk)

    lag = block_count - 1
    pending = None
    for now in range(CHUNKS + lag):
        if now < CHUNKS + lag - 1:
            forward(now)
        done = [g for g in GROUPS if g[0] + g[1] - 1 + lag == now]
        if not done:
            continue
        if done[0][0] == 0:
            for chunk in range(CHUNKS):
                relay_right(right, chunk, right_send, right_recv)
            split_right(right, 0, 0, blk)
            split_right(right, 2, 0, blk)
            for chunk in range(CHUNKS):
                wait_next(right, chunk, right_send, right_recv)
            split_right(right, 1, 0, blk)
        consume(*done[0])
        if pending:
            for chunk in range(pending[0], sum(pending)):
                relay_right(square, chunk, square_send, square_recv)
        pending = done[0]

    def accumulate(terms, last):
        def step(tile, carry):
            span = pl.ds(pl.multiple_of(tile * ROW_TILE, ROW_TILE), ROW_TILE)
            total = cube[span, :] if last else jnp.zeros((ROW_TILE, half_cols), jnp.float32)
            for section, side in terms:
                depth = slice(side * half_cols, (side + 1) * half_cols)
                total = total + product(
                    left_high[section, side, span, :], left_low[section, side, span, :],
                    right_high[section, depth, :], right_low[section, depth, :],
                )
            cube[span, :] = total
            return carry

        lax.fori_loop(0, blk // ROW_TILE, step, 0)

    split_right(square, 0, 0, blk)
    for chunk in range(CHUNKS // 2):
        wait_next(square, chunk, square_send, square_recv)
    split_right(square, 1, 0, half_cols)
    split_right(square, 2, 0, half_cols)
    accumulate([(0, 0), (0, 1), (1, 0), (2, 0)], False)
    relay_right(square, CHUNKS - 1, square_send, square_recv)
    split_right(square, 2, half_cols, half_cols)
    for chunk in range(CHUNKS // 2, CHUNKS):
        wait_next(square, chunk, square_send, square_recv)
    split_right(square, 1, half_cols, half_cols)
    accumulate([(1, 1), (2, 1)], True)

    for i in range(tile_rows):
        span = slice(i * tr, (i + 1) * tr)
        out_ref[span, :] = 3.0 * square[0, span, :] - 2.0 * masked_by_tiles(cube[span, :], i * tr)

    def all_sent(whole, send_sem):
        pltpu.make_async_copy(whole, whole, send_sem).wait()

    for section in range(SECTIONS):
        source = lax.rem(r + section, block_count)
        whole = left.at[section, half]

        @pl.when(jnp.logical_and(has_prev, source >= place))
        def _():
            all_sent(whole, z_send.at[0, section])

        @pl.when(jnp.logical_and(has_next, source <= place))
        def _():
            all_sent(whole, z_send.at[1, section])

        all_sent(whole, y_send.at[section])
    for sems in (right_send, square_send):
        for k in range(2):
            all_sent(right.at[0], sems.at[k])


def per_device(density, occupancy):
    blk, half_cols = density.shape
    row_count, col_count = lax.axis_size("row"), lax.axis_size("col")
    dma = pltpu.SemaphoreType.DMA
    wide = (SECTIONS, 2, blk, half_cols)
    tall = (SECTIONS, blk, half_cols)
    flops = 12 * blk * SECTIONS * blk * half_cols
    return pl.pallas_call(
        functools.partial(kernel, row_count, col_count),
        out_shape=jax.ShapeDtypeStruct(density.shape, jnp.float32),
        in_specs=[
            pl.BlockSpec(memory_space=pltpu.SMEM),
            pl.BlockSpec(memory_space=pltpu.HBM),
        ],
        out_specs=pl.BlockSpec(memory_space=pltpu.VMEM),
        scratch_shapes=[
            pltpu.VMEM(wide, jnp.float32),
            pltpu.VMEM(wide, jnp.bfloat16),
            pltpu.VMEM(wide, jnp.bfloat16),
            pltpu.VMEM(tall, jnp.float32),
            pltpu.VMEM(tall, jnp.float32),
            pltpu.VMEM(tall, jnp.bfloat16),
            pltpu.VMEM(tall, jnp.bfloat16),
            pltpu.VMEM((blk, half_cols), jnp.float32),
            dma((SECTIONS, 2, CHUNKS)),
            dma((2, SECTIONS)),
            dma((SECTIONS,)),
            dma((2, CHUNKS)),
            dma((2,)),
            dma((2, CHUNKS)),
            dma((2,)),
            dma,
        ],
        compiler_params=pltpu.CompilerParams(
            collective_id=0, has_side_effects=True, vmem_limit_bytes=53 * 2**20
        ),
        cost_estimate=pl.CostEstimate(
            flops=flops, bytes_accessed=2 * 4 * blk * half_cols, transcendentals=0
        ),
    )(occupancy.T, density)


def solution(mesh):
    in_specs = (P("row", "col"), P("row", "col"))
    out_specs = P("row", "col")
    return jax.shard_map(
        per_device, mesh=mesh, in_specs=in_specs, out_specs=out_specs, check_vma=False
    )
```

```python
import functools

import jax
import jax.numpy as jnp
from jax import lax
from jax.experimental import pallas as pl
from jax.experimental.pallas import tpu as pltpu
from jax.sharding import PartitionSpec as P

SECTIONS = 3
CHUNKS = 8
GROUPS = ((0, 2), (2, 2), (4, 2), (6, 1), (7, 1))
AHEAD = 2
ROW_TILE = 128
MESH = pl.DeviceIdType.MESH


def split(values):
    high = values.astype(jnp.bfloat16)
    low = (values - high.astype(jnp.float32)).astype(jnp.bfloat16)
    return high, low


def product(left_high, left_low, right_high, right_low):
    dot = functools.partial(jnp.dot, preferred_element_type=jnp.float32)
    count = left_high.shape[0]
    both = dot(jnp.concatenate([left_high, left_low], axis=0), right_high)
    return both[:count] + (both[count:] + dot(left_high, right_low))


def kernel(
    row_count, col_count, occ_ref, den_ref, out_ref,
    left, left_high, left_low, right, square, right_high, right_low, cube,
    left_recv, z_send, y_send, right_recv, right_send, square_recv, square_send, load_sem,
):
    blk, half_cols = den_ref.shape
    rows = blk // CHUNKS
    tile_cols, tile_rows = occ_ref.shape
    tr, tc = blk // tile_rows, half_cols // tile_cols
    block_count = col_count // 2

    r, c = lax.axis_index("row"), lax.axis_index("col")
    place, half = lax.div(c, 2), lax.rem(c, 2)
    other = 1 - half
    core = lax.rem(r, 2)
    partner = c + 1 - 2 * half
    buddy = r + 1 - 2 * core
    above = lax.rem(r + row_count - 2, row_count)
    below = lax.rem(r + 2, row_count)
    has_prev, has_next = place > 0, place < block_count - 1
    own_section = lax.rem(place - r + block_count, block_count)

    load = pltpu.make_async_copy(den_ref, cube, load_sem)
    load.start()

    barrier = pltpu.get_barrier_semaphore()

    def greet(**device):
        pl.semaphore_signal(barrier, inc=1, device_id=device, device_id_type=MESH)

    @pl.when(has_prev)
    def _():
        greet(col=c - 2)

    @pl.when(has_next)
    def _():
        greet(col=c + 2)

    greet(col=partner)
    greet(row=buddy)
    greet(row=above)
    if row_count > 4:
        greet(row=below)

    def masked_by_tiles(values, first_row):
        count = min(tr, values.shape[0])
        lines = []
        for i in range(0, values.shape[0], count):
            line = []
            for k in range(tile_cols):
                weight = occ_ref[k, (first_row + i) // tr].astype(jnp.float32)
                line.append(values[i : i + count, k * tc : (k + 1) * tc] * weight)
            lines.append(jnp.concatenate(line, axis=1))
        return jnp.concatenate(lines, axis=0)

    load.wait()
    for i in range(tile_rows):
        part = masked_by_tiles(cube[i * tr : (i + 1) * tr, :], i * tr)
        right[0, i * tr : (i + 1) * tr, :] = part

        @pl.when(own_section < SECTIONS)
        def _():
            left[own_section, half, i * tr : (i + 1) * tr, :] = part

    pl.semaphore_wait(
        barrier,
        has_prev.astype(jnp.int32) + has_next.astype(jnp.int32) + (4 if row_count > 4 else 3),
    )

    def left_copy(section, side, chunk, send_sem, **device):
        piece = left.at[section, side, pl.ds(chunk * rows, rows), :]
        return pltpu.make_async_remote_copy(
            src_ref=piece, dst_ref=piece, send_sem=send_sem,
            recv_sem=left_recv.at[section, side, chunk],
            device_id=device, device_id_type=MESH,
        )

    def spread(section, chunk, to_prev, to_next):
        if to_prev:
            @pl.when(has_prev)
            def _():
                left_copy(section, half, chunk, z_send.at[0, section], col=c - 2).start()

        if to_next:
            @pl.when(has_next)
            def _():
                left_copy(section, half, chunk, z_send.at[1, section], col=c + 2).start()

        left_copy(section, half, chunk, y_send.at[section], col=partner).start()

    def wait_left(section, side, chunk):
        left_copy(section, side, chunk, y_send.at[section], col=partner).wait_recv()

    def send_own(chunk):
        @pl.when(own_section < SECTIONS)
        def _():
            spread(own_section, chunk, True, True)

    def forward(now):
        if now + AHEAD < CHUNKS:
            send_own(now + AHEAD)

        nearest, furthest = max(1, now + 2 - CHUNKS), min(block_count - 1, now + 1)

        def step(index, carry):
            distance = nearest + furthest - index
            chunk = now + 1 - distance
            for sign in (-1, 1):
                source = place + sign * distance
                section = lax.rem(source - r + 2 * block_count, block_count)
                inside = source >= 0 if sign < 0 else source < block_count

                @pl.when(jnp.logical_and(inside, section < SECTIONS))
                def _():
                    wait_left(section, half, chunk)
                    spread(section, chunk, sign > 0, sign < 0)

            return carry

        lax.fori_loop(nearest, furthest + 1, step, 0)

    def right_copy(buffer, from_slot, to_slot, chunk, send_sem, recv_sems, device_row):
        span = pl.ds(chunk * rows, rows)
        return pltpu.make_async_remote_copy(
            src_ref=buffer.at[from_slot, span, :], dst_ref=buffer.at[to_slot, span, :],
            send_sem=send_sem, recv_sem=recv_sems.at[to_slot - 1, chunk],
            device_id={"row": device_row}, device_id_type=MESH,
        )

    def send_right(buffer, chunk, send_sems, recv_sems):
        right_copy(buffer, 0, 2, chunk, send_sems.at[0], recv_sems, above).start()

        @pl.when(core == 1)
        def _():
            right_copy(buffer, 0, 1, chunk, send_sems.at[1], recv_sems, buddy).start()

    def relay_right(buffer, chunk, send_sems, recv_sems):
        right_copy(buffer, 0, 2, chunk, send_sems.at[0], recv_sems, above).wait_recv()

        @pl.when(core == 0)
        def _():
            right_copy(buffer, 2, 1, chunk, send_sems.at[1], recv_sems, buddy).start()

    def wait_next(buffer, chunk, send_sems, recv_sems):
        right_copy(buffer, 0, 1, chunk, send_sems.at[1], recv_sems, buddy).wait_recv()

    def split_right(buffer, slot, first, count):
        high, low = split(buffer[slot, first : first + count, :])
        right_high[slot, first : first + count, :] = high
        right_low[slot, first : first + count, :] = low

    def consume(first, count):
        span = slice(first * rows, (first + count) * rows)
        for chunk in range(first, first + count):
            for section in range(SECTIONS):
                wait_left(section, other, chunk)
        total = jnp.zeros((count * rows, half_cols), jnp.float32)
        for section in range(SECTIONS):
            for side in range(2):
                high, low = split(left[section, side, span, :])
                left_high[section, side, span, :] = high
                left_low[section, side, span, :] = low
                depth = slice(side * half_cols, (side + 1) * half_cols)
                total = total + product(
                    high, low, right_high[section, depth, :], right_low[section, depth, :]
                )
        square[0, span, :] = masked_by_tiles(total, first * rows)
        for chunk in range(first, first + count):
            send_right(square, chunk, square_send, square_recv)

    for chunk in range(CHUNKS):
        send_right(right, chunk, right_send, right_recv)
    for chunk in range(AHEAD):
        send_own(chunk)

    lag = block_count - 1
    pending = None
    for now in range(CHUNKS + lag):
        if now < CHUNKS + lag - 1:
            forward(now)
        done = [g for g in GROUPS if g[0] + g[1] - 1 + lag == now]
        if not done:
            continue
        if done[0][0] == 0:
            for chunk in range(CHUNKS):
                relay_right(right, chunk, right_send, right_recv)
            split_right(right, 0, 0, blk)
            split_right(right, 2, 0, blk)
            for chunk in range(CHUNKS):
                wait_next(right, chunk, right_send, right_recv)
            split_right(right, 1, 0, blk)
        consume(*done[0])
        if pending:
            for chunk in range(pending[0], sum(pending)):
                relay_right(square, chunk, square_send, square_recv)
        pending = done[0]

    def accumulate(terms, last):
        def step(tile, carry):
            span = pl.ds(pl.multiple_of(tile * ROW_TILE, ROW_TILE), ROW_TILE)
            total = cube[span, :] if last else jnp.zeros((ROW_TILE, half_cols), jnp.float32)
            for section, side in terms:
                depth = slice(side * half_cols, (side + 1) * half_cols)
                total = total + product(
                    left_high[section, side, span, :], left_low[section, side, span, :],
                    right_high[section, depth, :], right_low[section, depth, :],
                )
            cube[span, :] = total
            return carry

        lax.fori_loop(0, blk // ROW_TILE, step, 0)

    split_right(square, 0, 0, blk)
    for chunk in range(CHUNKS // 2):
        wait_next(square, chunk, square_send, square_recv)
    split_right(square, 1, 0, half_cols)
    split_right(square, 2, 0, half_cols)
    accumulate([(0, 0), (0, 1), (1, 0), (2, 0)], False)
    relay_right(square, CHUNKS - 1, square_send, square_recv)
    split_right(square, 2, half_cols, half_cols)
    for chunk in range(CHUNKS // 2, CHUNKS):
        wait_next(square, chunk, square_send, square_recv)
    split_right(square, 1, half_cols, half_cols)
    accumulate([(1, 1), (2, 1)], True)

    for i in range(tile_rows):
        span = slice(i * tr, (i + 1) * tr)
        out_ref[span, :] = 3.0 * square[0, span, :] - 2.0 * masked_by_tiles(cube[span, :], i * tr)

    def all_sent(whole, send_sem):
        pltpu.make_async_copy(whole, whole, send_sem).wait()

    for section in range(SECTIONS):
        source = lax.rem(r + section, block_count)
        whole = left.at[section, half]

        @pl.when(jnp.logical_and(has_prev, source >= place))
        def _():
            all_sent(whole, z_send.at[0, section])

        @pl.when(jnp.logical_and(has_next, source <= place))
        def _():
            all_sent(whole, z_send.at[1, section])

        all_sent(whole, y_send.at[section])
    for sems in (right_send, square_send):
        for k in range(2):
            all_sent(right.at[0], sems.at[k])


def per_device(density, occupancy):
    blk, half_cols = density.shape
    row_count, col_count = lax.axis_size("row"), lax.axis_size("col")
    dma = pltpu.SemaphoreType.DMA
    wide = (SECTIONS, 2, blk, half_cols)
    tall = (SECTIONS, blk, half_cols)
    flops = 12 * blk * SECTIONS * blk * half_cols
    return pl.pallas_call(
        functools.partial(kernel, row_count, col_count),
        out_shape=jax.ShapeDtypeStruct(density.shape, jnp.float32),
        in_specs=[
            pl.BlockSpec(memory_space=pltpu.SMEM),
            pl.BlockSpec(memory_space=pltpu.HBM),
        ],
        out_specs=pl.BlockSpec(memory_space=pltpu.VMEM),
        scratch_shapes=[
            pltpu.VMEM(wide, jnp.float32),
            pltpu.VMEM(wide, jnp.bfloat16),
            pltpu.VMEM(wide, jnp.bfloat16),
            pltpu.VMEM(tall, jnp.float32),
            pltpu.VMEM(tall, jnp.float32),
            pltpu.VMEM(tall, jnp.bfloat16),
            pltpu.VMEM(tall, jnp.bfloat16),
            pltpu.VMEM((blk, half_cols), jnp.float32),
            dma((SECTIONS, 2, CHUNKS)),
            dma((2, SECTIONS)),
            dma((SECTIONS,)),
            dma((2, CHUNKS)),
            dma((2,)),
            dma((2, CHUNKS)),
            dma((2,)),
            dma,
        ],
        compiler_params=pltpu.CompilerParams(
            collective_id=0, has_side_effects=True, vmem_limit_bytes=53 * 2**20
        ),
        cost_estimate=pl.CostEstimate(
            flops=flops, bytes_accessed=2 * 4 * blk * half_cols, transcendentals=0
        ),
    )(occupancy.T, density)


def solution(mesh):
    in_specs = (P("row", "col"), P("row", "col"))
    out_specs = P("row", "col")
    return jax.shard_map(
        per_device, mesh=mesh, in_specs=in_specs, out_specs=out_specs, check_vma=False
    )
```

```python
import functools

import jax
import jax.numpy as jnp
from jax import lax
from jax.experimental import pallas as pl
from jax.experimental.pallas import tpu as pltpu
from jax.sharding import PartitionSpec as P

SECTIONS = 3
CHUNKS = 8
GROUPS = ((0, 2), (2, 2), (4, 2), (6, 1), (7, 1))
AHEAD = 2
ROW_TILE = 128
MESH = pl.DeviceIdType.MESH


def split(values):
    high = values.astype(jnp.bfloat16)
    low = (values - high.astype(jnp.float32)).astype(jnp.bfloat16)
    return high, low


def product(left_high, left_low, right_high, right_low):
    dot = functools.partial(jnp.dot, preferred_element_type=jnp.float32)
    count = left_high.shape[0]
    both = dot(jnp.concatenate([left_high, left_low], axis=0), right_high)
    return both[:count] + (both[count:] + dot(left_high, right_low))


def kernel(
    row_count, col_count, occ_ref, den_ref, out_ref,
    left, left_high, left_low, right, square, right_high, right_low, cube,
    left_recv, z_send, y_send, right_recv, right_send, square_recv, square_send, load_sem,
):
    blk, half_cols = den_ref.shape
    rows = blk // CHUNKS
    tile_cols, tile_rows = occ_ref.shape
    tr, tc = blk // tile_rows, half_cols // tile_cols
    block_count = col_count // 2

    r, c = lax.axis_index("row"), lax.axis_index("col")
    place, half = lax.div(c, 2), lax.rem(c, 2)
    other = 1 - half
    core = lax.rem(r, 2)
    partner = c + 1 - 2 * half
    buddy = r + 1 - 2 * core
    above = lax.rem(r + row_count - 2, row_count)
    below = lax.rem(r + 2, row_count)
    has_prev, has_next = place > 0, place < block_count - 1
    own_section = lax.rem(place - r + block_count, block_count)

    load = pltpu.make_async_copy(den_ref, cube, load_sem)
    load.start()

    barrier = pltpu.get_barrier_semaphore()

    def greet(**device):
        pl.semaphore_signal(barrier, inc=1, device_id=device, device_id_type=MESH)

    @pl.when(has_prev)
    def _():
        greet(col=c - 2)

    @pl.when(has_next)
    def _():
        greet(col=c + 2)

    greet(col=partner)
    greet(row=buddy)
    greet(row=above)
    if row_count > 4:
        greet(row=below)

    def masked_by_tiles(values, first_row):
        count = min(tr, values.shape[0])
        lines = []
        for i in range(0, values.shape[0], count):
            line = []
            for k in range(tile_cols):
                weight = occ_ref[k, (first_row + i) // tr].astype(jnp.float32)
                line.append(values[i : i + count, k * tc : (k + 1) * tc] * weight)
            lines.append(jnp.concatenate(line, axis=1))
        return jnp.concatenate(lines, axis=0)

    load.wait()
    for i in range(tile_rows):
        part = masked_by_tiles(cube[i * tr : (i + 1) * tr, :], i * tr)
        right[0, i * tr : (i + 1) * tr, :] = part

        @pl.when(own_section < SECTIONS)
        def _():
            left[own_section, half, i * tr : (i + 1) * tr, :] = part

    pl.semaphore_wait(
        barrier,
        has_prev.astype(jnp.int32) + has_next.astype(jnp.int32) + (4 if row_count > 4 else 3),
    )

    def left_copy(section, side, chunk, send_sem, **device):
        piece = left.at[section, side, pl.ds(chunk * rows, rows), :]
        return pltpu.make_async_remote_copy(
            src_ref=piece, dst_ref=piece, send_sem=send_sem,
            recv_sem=left_recv.at[section, side, chunk],
            device_id=device, device_id_type=MESH,
        )

    def spread(section, chunk, to_prev, to_next):
        if to_prev:
            @pl.when(has_prev)
            def _():
                left_copy(section, half, chunk, z_send.at[0, section], col=c - 2).start()

        if to_next:
            @pl.when(has_next)
            def _():
                left_copy(section, half, chunk, z_send.at[1, section], col=c + 2).start()

        left_copy(section, half, chunk, y_send.at[section], col=partner).start()

    def wait_left(section, side, chunk):
        left_copy(section, side, chunk, y_send.at[section], col=partner).wait_recv()

    def send_own(chunk):
        @pl.when(own_section < SECTIONS)
        def _():
            spread(own_section, chunk, True, True)

    def forward(now):
        nearest, furthest = max(1, now + 2 - CHUNKS), min(block_count - 1, now + 1)

        def step(index, carry):
            distance = nearest + furthest - index
            chunk = now + 1 - distance
            for sign in (-1, 1):
                source = place + sign * distance
                section = lax.rem(source - r + 2 * block_count, block_count)
                inside = source >= 0 if sign < 0 else source < block_count

                @pl.when(jnp.logical_and(inside, section < SECTIONS))
                def _():
                    wait_left(section, half, chunk)
                    spread(section, chunk, sign > 0, sign < 0)

            return carry

        lax.fori_loop(nearest, furthest + 1, step, 0)
        if now + AHEAD < CHUNKS:
            send_own(now + AHEAD)

    def right_copy(buffer, from_slot, to_slot, chunk, send_sem, recv_sems, device_row):
        span = pl.ds(chunk * rows, rows)
        return pltpu.make_async_remote_copy(
            src_ref=buffer.at[from_slot, span, :], dst_ref=buffer.at[to_slot, span, :],
            send_sem=send_sem, recv_sem=recv_sems.at[to_slot - 1, chunk],
            device_id={"row": device_row}, device_id_type=MESH,
        )

    def send_right(buffer, chunk, send_sems, recv_sems):
        right_copy(buffer, 0, 2, chunk, send_sems.at[0], recv_sems, above).start()

        @pl.when(core == 1)
        def _():
            right_copy(buffer, 0, 1, chunk, send_sems.at[1], recv_sems, buddy).start()

    def relay_right(buffer, chunk, send_sems, recv_sems):
        right_copy(buffer, 0, 2, chunk, send_sems.at[0], recv_sems, above).wait_recv()

        @pl.when(core == 0)
        def _():
            right_copy(buffer, 2, 1, chunk, send_sems.at[1], recv_sems, buddy).start()

    def wait_next(buffer, chunk, send_sems, recv_sems):
        right_copy(buffer, 0, 1, chunk, send_sems.at[1], recv_sems, buddy).wait_recv()

    def split_right(buffer, slot, first, count):
        high, low = split(buffer[slot, first : first + count, :])
        right_high[slot, first : first + count, :] = high
        right_low[slot, first : first + count, :] = low

    def consume(first, count):
        span = slice(first * rows, (first + count) * rows)
        for chunk in range(first, first + count):
            for section in range(SECTIONS):
                wait_left(section, other, chunk)
        total = jnp.zeros((count * rows, half_cols), jnp.float32)
        for section in range(SECTIONS):
            for side in range(2):
                high, low = split(left[section, side, span, :])
                left_high[section, side, span, :] = high
                left_low[section, side, span, :] = low
                depth = slice(side * half_cols, (side + 1) * half_cols)
                total = total + product(
                    high, low, right_high[section, depth, :], right_low[section, depth, :]
                )
        square[0, span, :] = masked_by_tiles(total, first * rows)
        for chunk in range(first, first + count):
            send_right(square, chunk, square_send, square_recv)

    for chunk in range(CHUNKS):
        send_right(right, chunk, right_send, right_recv)
    for chunk in range(AHEAD):
        send_own(chunk)

    lag = block_count - 1
    pending = None
    for now in range(CHUNKS + lag):
        if now < CHUNKS + lag - 1:
            forward(now)
        done = [g for g in GROUPS if g[0] + g[1] - 1 + lag == now]
        if not done:
            continue
        if done[0][0] == 0:
            for chunk in range(CHUNKS):
                relay_right(right, chunk, right_send, right_recv)
            split_right(right, 0, 0, blk)
            split_right(right, 2, 0, blk)
            for chunk in range(CHUNKS):
                wait_next(right, chunk, right_send, right_recv)
            split_right(right, 1, 0, blk)
        consume(*done[0])
        if pending:
            for chunk in range(pending[0], sum(pending)):
                relay_right(square, chunk, square_send, square_recv)
        pending = done[0]

    def accumulate(terms, last):
        def step(tile, carry):
            span = pl.ds(pl.multiple_of(tile * ROW_TILE, ROW_TILE), ROW_TILE)
            total = cube[span, :] if last else jnp.zeros((ROW_TILE, half_cols), jnp.float32)
            for section, side in terms:
                depth = slice(side * half_cols, (side + 1) * half_cols)
                total = total + product(
                    left_high[section, side, span, :], left_low[section, side, span, :],
                    right_high[section, depth, :], right_low[section, depth, :],
                )
            cube[span, :] = total
            return carry

        lax.fori_loop(0, blk // ROW_TILE, step, 0)

    split_right(square, 0, 0, blk)
    for chunk in range(CHUNKS // 2):
        wait_next(square, chunk, square_send, square_recv)
    split_right(square, 1, 0, half_cols)
    split_right(square, 2, 0, half_cols)
    accumulate([(0, 0), (0, 1), (1, 0), (2, 0)], False)
    relay_right(square, CHUNKS - 1, square_send, square_recv)
    split_right(square, 2, half_cols, half_cols)
    for chunk in range(CHUNKS // 2, CHUNKS):
        wait_next(square, chunk, square_send, square_recv)
    split_right(square, 1, half_cols, half_cols)
    accumulate([(1, 1), (2, 1)], True)

    for i in range(tile_rows):
        span = slice(i * tr, (i + 1) * tr)
        out_ref[span, :] = 3.0 * square[0, span, :] - 2.0 * masked_by_tiles(cube[span, :], i * tr)

    def all_sent(whole, send_sem):
        pltpu.make_async_copy(whole, whole, send_sem).wait()

    for section in range(SECTIONS):
        source = lax.rem(r + section, block_count)
        whole = left.at[section, half]

        @pl.when(jnp.logical_and(has_prev, source >= place))
        def _():
            all_sent(whole, z_send.at[0, section])

        @pl.when(jnp.logical_and(has_next, source <= place))
        def _():
            all_sent(whole, z_send.at[1, section])

        all_sent(whole, y_send.at[section])
    for sems in (right_send, square_send):
        for k in range(2):
            all_sent(right.at[0], sems.at[k])


def per_device(density, occupancy):
    blk, half_cols = density.shape
    row_count, col_count = lax.axis_size("row"), lax.axis_size("col")
    dma = pltpu.SemaphoreType.DMA
    wide = (SECTIONS, 2, blk, half_cols)
    tall = (SECTIONS, blk, half_cols)
    flops = 12 * blk * SECTIONS * blk * half_cols
    return pl.pallas_call(
        functools.partial(kernel, row_count, col_count),
        out_shape=jax.ShapeDtypeStruct(density.shape, jnp.float32),
        in_specs=[
            pl.BlockSpec(memory_space=pltpu.SMEM),
            pl.BlockSpec(memory_space=pltpu.HBM),
        ],
        out_specs=pl.BlockSpec(memory_space=pltpu.VMEM),
        scratch_shapes=[
            pltpu.VMEM(wide, jnp.float32),
            pltpu.VMEM(wide, jnp.bfloat16),
            pltpu.VMEM(wide, jnp.bfloat16),
            pltpu.VMEM(tall, jnp.float32),
            pltpu.VMEM(tall, jnp.float32),
            pltpu.VMEM(tall, jnp.bfloat16),
            pltpu.VMEM(tall, jnp.bfloat16),
            pltpu.VMEM((blk, half_cols), jnp.float32),
            dma((SECTIONS, 2, CHUNKS)),
            dma((2, SECTIONS)),
            dma((SECTIONS,)),
            dma((2, CHUNKS)),
            dma((2,)),
            dma((2, CHUNKS)),
            dma((2,)),
            dma,
        ],
        compiler_params=pltpu.CompilerParams(
            collective_id=0, has_side_effects=True, vmem_limit_bytes=53 * 2**20
        ),
        cost_estimate=pl.CostEstimate(
            flops=flops, bytes_accessed=2 * 4 * blk * half_cols, transcendentals=0
        ),
    )(occupancy.T, density)


def solution(mesh):
    in_specs = (P("row", "col"), P("row", "col"))
    out_specs = P("row", "col")
    return jax.shard_map(
        per_device, mesh=mesh, in_specs=in_specs, out_specs=out_specs, check_vma=False
    )
```
